128 devices in a mesh: gx: 8 (over z, core), gy: 16 (over y, x).
Axes of the slice: x: 4, y: 4, z: 4, core: 2. Of those that a mesh axis runs over, the one named last changes fastest.
Arguments:
- populations: float32 [19, 64, 16384], P(None, 'gx', 'gy'), may hold values from 0.02 to 0.08
- solid: int32 [64, 16384], P('gx', 'gy'), may hold values 0 or 1
- link_cell: int32 [2097152], P(('gx', 'gy')), may hold values from 0 to 8191
- link_dir: int32 [2097152], P(('gx', 'gy')), may hold values from 1 to 18
- link_owner: int32 [2097152, 1], P(('gx', 'gy')), may hold values from 0 to 127; in each aligned block of 16384 rows (0 to 16383, 16384 to 32767, ...) at most 512 rows name the same one
- link_elem: int32 [2097152], P(('gx', 'gy')), may hold values from 0 to 4095
- elem_nodes: int32 [3, 524288], P(None, ('gx', 'gy')), may hold values from 0 to 2559
- elem_grads: float32 [6, 524288], P(None, ('gx', 'gy')), may hold values from -6 to 6
- elem_area: float32 [524288], P(('gx', 'gy')), may hold values from 0.005 to 0.02
- elem_normal: float32 [3, 524288], P(None, ('gx', 'gy')), may hold values from -1 to 1
- node_mass: float32 [262144], P(('gx', 'gy')), may hold values from 0.05 to 0.5
- displacement: float32 [262144], P(('gx', 'gy')), may hold values from -6 to 6
- velocity: float32 [262144], P(('gx', 'gy')), may hold values from -3 to 3
Outputs:
- populations_out: float32 [19, 64, 16384], P(None, 'gx', 'gy')
- element_force: float32 [3, 524288], P(None, ('gx', 'gy'))
- displacement_out: float32 [262144], P(('gx', 'gy'))
- velocity_out: float32 [262144], P(('gx', 'gy'))
The draws below stay inside these ranges and needn't reach their ends.
Inputs may be any that keep to these rules, and one draw needn't show every extreme that they name: `link_owner`: in each device's 16384 rows no owner is named more than 512 times, a bound that some block reaches. `link_cell`: A cell of the block of the device that holds the link. `elem_nodes`: values 2048 and above name the first 512 nodes of the next device along gx+gy, the last device's next being the first.
All inputs are finite; a program needn't handle non-finite values. No bound on the sum of `solid` on one device may be relied on, other than what follows from the above.
Results may differ from the reference program's by a relative error of at most 0.00002.
Values sent between devices are 32-bit elements; how exact they have to be, the bound alone decides.
A program may use at most 128 MiB of HBM per device.

```python
import math
import jax
import jax.numpy as jnp
import numpy as np

CX = 8
CY = 16
NZ = 64
LINKS_DEV = 16384
ELEM_DEV = 4096
RIM = 512
OWNERS = 128
NODE_DEV = 2048
CAP = 512
NX = 64
NY = 256
LINKS = 2097152
ELEMENTS = 524288
NODES = 262144
N_GY = 16


def set_ends(values, stream_key, smallest, top_value):
    dims = values.shape
    index_at = [jax.random.randint(jax.random.fold_in(stream_key, axis), (), 0, dims[axis]) for axis in range(len(dims))]
    values = values.at[tuple(index_at)].set(smallest)
    longest = dims.index(max(dims))
    index_at[longest] = (index_at[longest] + 1) % dims[longest]
    return values.at[tuple(index_at)].set(top_value)


def level_of(key, dims, cuts, smallest, high):
    gain, own = 1.0, jax.random.fold_in(key, 6)
    for position, blocks in cuts:
        steps = jnp.exp(jax.random.uniform(jax.random.fold_in(own, position), (blocks,), jnp.float32, smallest / len(cuts), high / len(cuts)))
        gain = gain * jnp.repeat(steps, dims[position] // blocks).reshape([-1 if axis == position else 1 for axis in range(len(dims))])
    return gain


def shared_out(rng, own, number, rows, number_of, top, bound, lean):
    order = jax.random.permutation(rng, number_of)
    crowded, ordinary = load_shares(number_of, rows * top, bound, lean, True), load_shares(number_of, rows * top, bound, lean, False)
    places = jnp.arange(number_of)

    def named(sizes, offset_by):
        used = int((sizes > 0).sum())
        fixed = max(1, used // 4)
        moved = fixed + (places - fixed + offset_by * (used - fixed)) % max(1, number_of - fixed)
        return jnp.zeros((number_of,), jnp.int32).at[order[jnp.where(places < fixed, places, moved)]].set(jnp.asarray(sizes, jnp.int32))

    sizes = jnp.where(number % 4 == 0, named(crowded, number // 4), named(ordinary, number - number // 4 - 1))
    mixed = jax.random.permutation(jax.random.fold_in(own, 3), number_of)
    source_of, taker = mixed[0:number_of // 2 * 2:2], mixed[1:number_of // 2 * 2:2]
    slack = jnp.minimum(sizes[source_of] - 1, bound - sizes[taker]) // 2
    slack = jnp.where((source_of == order[0]) | (taker == order[0]) | (sizes[taker] == 0), 0, jnp.maximum(slack, 0))
    moved = jax.random.randint(jax.random.fold_in(own, 4), (number_of // 2,), 0, 1 << 20) % (slack + 1)
    sizes = sizes.at[source_of].add(-moved).at[taker].add(moved)
    labels = jnp.searchsorted(jnp.cumsum(sizes), jnp.arange(rows * top), side="right").astype(jnp.int32)
    grid = labels.reshape(top, rows).T
    grid = grid[jax.random.permutation(jax.random.fold_in(own, 1), rows)]
    offset_by = jax.random.randint(jax.random.fold_in(own, 2), (rows, 1), 0, top)
    return jnp.take_along_axis(grid, (jnp.arange(top)[None, :] + offset_by) % top, axis=1)


def load_shares(count, total, most, slope, full):
    portions = [(1 << 20) // math.isqrt(standing ** slope) + 1 for standing in range(1, count + 1)]
    largest = most if full else min(most, max(-(-total // count), total * portions[0] // sum(portions)))
    least = 1 if total - largest >= count - 1 else 0
    given, spare = [largest] + [least] * (count - 1), total - largest - least * (count - 1)
    while spare > 0:
        free = [i for i in range(1, count) if given[i] < largest] or [i for i in range(1, count) if given[i] < most]
        whole, remaining = sum([portions[i] for i in free]), spare
        for i in free:
            extra = min(most - given[i], max(1, remaining * portions[i] // whole), spare)
            given[i] = given[i] + extra
            spare = spare - extra
    return np.array(given)


def scatter_about(stream_key, shape, scale, reach, split=(), kind=jnp.bfloat16):
    drawn = scale * jax.random.normal(stream_key, shape, jnp.float32)
    if split:
        drawn = drawn * level_of(stream_key, shape, split, -0.22, 0.18)
    return jnp.clip(drawn, -reach, reach).astype(kind)


def setup_inputs(seed: int = 0) -> dict:
    seeds = jax.random.split(jax.random.key(seed), 14)
    populations = jnp.clip(0.02 + 0.06 * jax.random.uniform(seeds[0], (19, NX, NY * NZ), jnp.float32) ** level_of(seeds[0], (19, NX, NY * NZ), ((1, 8), (2, 16)), -0.2, 0.2), 0.02, 0.08)
    solid = set_ends((jax.random.randint(seeds[1], (NX, NY * NZ), 0, 8) < 1).astype(jnp.int32), jax.random.fold_in(seeds[1], 1), 0, 1)
    link_cell = set_ends(jax.random.randint(seeds[2], (LINKS,), 0, CX * CY * NZ), jax.random.fold_in(seeds[2], 1), 0, (CX * CY * NZ) - 1).astype(jnp.int32)
    link_dir = set_ends(jax.random.randint(seeds[3], (LINKS,), 1, 19), jax.random.fold_in(seeds[3], 1), 1, 18).astype(jnp.int32)
    link_owner_keys = jax.random.split(jax.random.fold_in(seeds[4], 1), LINKS // LINKS_DEV)
    link_owner_turns = jax.random.permutation(jax.random.fold_in(seeds[4], 3), LINKS // LINKS_DEV)
    link_owner = jax.vmap(lambda own, number: shared_out(jax.random.fold_in(seeds[4], 2), own, number, LINKS_DEV, OWNERS, 1, CAP, 2))(link_owner_keys, link_owner_turns).reshape((LINKS, 1))
    link_elem = set_ends(jax.random.randint(seeds[5], (LINKS,), 0, ELEM_DEV), jax.random.fold_in(seeds[5], 1), 0, ELEM_DEV - 1).astype(jnp.int32)
    elem_nodes = set_ends(jax.random.randint(seeds[6], (3, ELEMENTS), 0, NODE_DEV + RIM), jax.random.fold_in(seeds[6], 1), 0, (NODE_DEV + RIM) - 1).astype(jnp.int32)
    elem_grads = scatter_about(seeds[7], (6, ELEMENTS), 1.0, 6.0, ((1, 128),), jnp.float32)
    elem_area = jnp.clip(0.005 + 0.015 * jax.random.uniform(seeds[8], (ELEMENTS,), jnp.float32) ** level_of(seeds[8], (ELEMENTS,), ((0, 128),), -0.2, 0.2), 0.005, 0.02)
    elem_normal = jnp.clip(jax.random.uniform(seeds[9], (3, ELEMENTS), jnp.float32, -1.0, 1.0) * level_of(seeds[9], (3, ELEMENTS), ((1, 128),), -0.4, 0.0), -1.0, 1.0)
    node_mass = jnp.clip(jnp.exp(math.log(0.5) - 2.3025851 * jax.random.uniform(seeds[10], (NODES,), jnp.float32) ** level_of(seeds[10], (NODES,), ((0, 128),), -0.2, 0.2)), 0.05, 0.5)
    displacement = scatter_about(seeds[11], (NODES,), 1.0, 6.0, ((0, 128),), jnp.float32)
    velocity = scatter_about(seeds[12], (NODES,), 0.5, 3.0, ((0, 128),), jnp.float32)
    return {"populations": populations, "solid": solid, "link_cell": link_cell, "link_dir": link_dir, "link_owner": link_owner, "link_elem": link_elem, "elem_nodes": elem_nodes, "elem_grads": elem_grads, "elem_area": elem_area, "elem_normal": elem_normal, "node_mass": node_mass, "displacement": displacement, "velocity": velocity}


lattice_speeds = [(0, 0, 0), (1, 0, 0), (-1, 0, 0), (0, 1, 0), (0, -1, 0), (0, 0, 1), (0, 0, -1),
                  (1, 1, 0), (-1, -1, 0), (1, -1, 0), (-1, 1, 0), (1, 0, 1), (-1, 0, -1),
                  (1, 0, -1), (-1, 0, 1), (0, 1, 1), (0, -1, -1), (0, 1, -1), (0, -1, 1)]
lattice_weights = [1.0 / 3.0] + [1.0 / 18.0] * 6 + [1.0 / 36.0] * 12
opposite_index = [0, 2, 1, 4, 3, 6, 5, 8, 7, 10, 9, 12, 11, 14, 13, 16, 15, 18, 17]
relax_time = 0.8
time_step = 0.5


def collide(popul, is_solid):
    density = jnp.sum(popul, axis=0)
    flow = []
    for k in range(3):
        total = jnp.zeros(density.shape, jnp.float32)
        for i in range(19):
            if lattice_speeds[i][k] != 0:
                total = total + lattice_speeds[i][k] * popul[i]
        flow.append(total / density)
    square = flow[0] * flow[0] + flow[1] * flow[1] + flow[2] * flow[2]
    result = []
    for i in range(19):
        along = lattice_speeds[i][0] * flow[0] + lattice_speeds[i][1] * flow[1] + lattice_speeds[i][2] * flow[2]
        equil = lattice_weights[i] * density * (1.0 + 3.0 * along + 4.5 * along * along - 1.5 * square)
        relaxed = popul[i] - (popul[i] - equil) / relax_time
        result.append(jnp.where(is_solid, popul[i], relaxed))
    return jnp.stack(result)


def speed_along(dirs, k):
    total = jnp.zeros(dirs.shape, jnp.float32)
    for i in range(19):
        if lattice_speeds[i][k] != 0:
            total = total + lattice_speeds[i][k] * (dirs == i).astype(jnp.float32)
    return total


def element_terms(nodes, grads, area, load, field):
    values = [field[nodes[j]] for j in range(3)]
    slope_x = grads[0] * values[0] + grads[2] * values[1] + grads[4] * values[2]
    slope_y = grads[1] * values[0] + grads[3] * values[1] + grads[5] * values[2]
    return [load - area * (grads[2 * j] * slope_x + grads[2 * j + 1] * slope_y) for j in range(3)]


def reference(populations, solid, link_cell, link_dir, link_owner, link_elem, elem_nodes, elem_grads,
              elem_area, elem_normal, node_mass, displacement, velocity):
    popul = populations.reshape(19, NX, NY, NZ)
    is_solid = solid.reshape(NX, NY, NZ) != 0
    post = collide(popul, is_solid)
    height = jnp.arange(NZ, dtype=jnp.int32).reshape(1, 1, NZ)
    read = []
    for i in range(19):
        cx, cy, cz = lattice_speeds[i]
        source = jnp.roll(post[i], (cx, cy, cz), axis=(0, 1, 2))
        src_solid = jnp.roll(is_solid, (cx, cy, cz), axis=(0, 1, 2))
        wall = (height - cz < 0) | (height - cz >= NZ)
        blocked = src_solid | wall
        value = jnp.where(blocked, post[opposite_index[i]], source)
        read.append(jnp.where(is_solid, post[i], value))
    populations_out = jnp.stack(read).reshape(19, NX, NY * NZ)

    row_ids = jnp.arange(LINKS_DEV * OWNERS, dtype=jnp.int32)
    device = row_ids // LINKS_DEV
    block_x = device // N_GY
    block_y = device % N_GY
    local_a = link_cell // (CY * NZ)
    remain = link_cell % (CY * NZ)
    local_b = remain // NZ
    local_z = remain % NZ
    global_x = block_x * CX + local_a
    global_y = block_y * CY + local_b
    flat_cell = (global_x * NY + global_y) * NZ + local_z
    cells = NX * NY * NZ
    value = post.reshape(-1)[link_dir * cells + flat_cell]
    link_force = jnp.stack([2.0 * speed_along(link_dir, k) * value for k in range(3)])
    target = link_owner[:, 0] * ELEM_DEV + link_elem
    element_force = jax.ops.segment_sum(link_force.T, target, num_segments=ELEM_DEV * OWNERS).T

    elem_ids = jnp.arange(ELEM_DEV * OWNERS, dtype=jnp.int32)
    elem_device = elem_ids // ELEM_DEV
    next_device = (elem_device + 1) % OWNERS
    global_nodes = jnp.where(elem_nodes < NODE_DEV, elem_device * NODE_DEV + elem_nodes,
                             next_device * NODE_DEV + elem_nodes - NODE_DEV)
    load = (elem_normal[0] * element_force[0] + elem_normal[1] * element_force[1]
            + elem_normal[2] * element_force[2]) / 3.0
    terms = element_terms(global_nodes, elem_grads, elem_area, load, displacement)
    node_force = jax.ops.segment_sum(jnp.concatenate(terms), global_nodes.reshape(-1),
                                     num_segments=NODE_DEV * OWNERS)
    velocity_out = velocity + time_step * node_force / node_mass
    displacement_out = displacement + time_step * velocity_out
    return populations_out, element_force, displacement_out, velocity_out
```

```python
import functools

import jax
import jax.numpy as jnp
from jax import lax
from jax.experimental import pallas as pl
from jax.experimental.pallas import tpu as pltpu
from jax.sharding import PartitionSpec as P

NZ = 64
RIM = 512
BLANK = -1e30

SPEEDS = [
    (0, 0, 0),
    (1, 0, 0),
    (-1, 0, 0),
    (0, 1, 0),
    (0, -1, 0),
    (0, 0, 1),
    (0, 0, -1),
    (1, 1, 0),
    (-1, -1, 0),
    (1, -1, 0),
    (-1, 1, 0),
    (1, 0, 1),
    (-1, 0, -1),
    (1, 0, -1),
    (-1, 0, 1),
    (0, 1, 1),
    (0, -1, -1),
    (0, 1, -1),
    (0, -1, 1),
]
WEIGHTS = [1.0 / 3.0] + [1.0 / 18.0] * 6 + [1.0 / 36.0] * 12
OPP = [0, 2, 1, 4, 3, 6, 5, 8, 7, 10, 9, 12, 11, 14, 13, 16, 15, 18, 17]
X_UP = [i for i in range(19) if SPEEDS[i][0] == 1]
X_DOWN = [i for i in range(19) if SPEEDS[i][0] == -1]
Y_UP = [i for i in range(19) if SPEEDS[i][1] == 1]
Y_DOWN = [i for i in range(19) if SPEEDS[i][1] == -1]
relax_time = 0.8
time_step = 0.5
VMEM = 48 * 1024 * 1024
F32 = jnp.float32
BF16 = jnp.bfloat16


def halves(x):
    high = x.astype(BF16)
    return high, (x - high.astype(F32)).astype(BF16)


def signed_sum(terms):
    plus = [v for s, v in terms if s > 0]
    minus = [v for s, v in terms if s < 0]
    return functools.reduce(jnp.add, plus) - functools.reduce(jnp.add, minus)


def collide_kernel(popul_ref, solid_ref, post_ref, table_ref):
    columns = popul_ref.shape[2]
    for t in range(columns // 128):
        at = pl.ds(128 * t, 128)
        f = [popul_ref[i, :, at] for i in range(19)]
        is_solid = solid_ref[:, at] != 0
        density = functools.reduce(jnp.add, f)
        inverse = 1.0 / density
        flow = [
            signed_sum([(SPEEDS[i][k], f[i]) for i in range(19) if SPEEDS[i][k] != 0]) * inverse
            for k in range(3)
        ]
        square = flow[0] * flow[0] + flow[1] * flow[1] + flow[2] * flow[2]
        rest = 1.0 - 1.5 * square
        keep = 1.0 - 1.0 / relax_time
        for i in range(19):
            if i != 0 and OPP[i] < i:
                continue
            scaled = (WEIGHTS[i] / relax_time) * density
            if i == 0:
                new = keep * f[0] + scaled * rest
                post_ref[0, :, at] = jnp.where(is_solid, f[0], new)
                continue
            along = signed_sum_any([(SPEEDS[i][k], flow[k]) for k in range(3) if SPEEDS[i][k] != 0])
            even = scaled * (rest + 4.5 * along * along)
            odd = scaled * (3.0 * along)
            j = OPP[i]
            post_ref[i, :, at] = jnp.where(is_solid, f[i], keep * f[i] + (even + odd))
            post_ref[j, :, at] = jnp.where(is_solid, f[j], keep * f[j] + (even - odd))
    for pair in range(9):
        block = jnp.concatenate(
            [
                post_ref[d, :, 128 * t : 128 * t + 128]
                for d in (1 + 2 * pair, 2 + 2 * pair)
                for t in range(columns // 128)
            ],
            axis=0,
        )
        high, low = halves(block.T)
        table_ref[0:128, 128 * pair : 128 * pair + 128] = high
        table_ref[128:256, 128 * pair : 128 * pair + 128] = low


def signed_sum_any(terms):
    total = None
    for s, v in terms:
        if total is None:
            total = v if s > 0 else -v
        else:
            total = total + v if s > 0 else total - v
    return total


def one_hot(index, size):
    rows = lax.broadcasted_iota(jnp.int32, (size, index.shape[1]), 0)
    return (rows == index).astype(F32).astype(BF16)


def links_kernel(starts_ref, key_ref, load_ref, table_ref, value_ref, where_ref, val_s, elem_s, dir_s):
    count = key_ref.shape[0]
    owners = value_ref.shape[0]

    def gather(b, carry):
        code = load_ref[pl.ds(2 * b, 2), :]
        code = jnp.concatenate([code[0:1], code[1:2]], axis=1)
        cell = code & 8191
        way = code >> 13
        row = (way - 1) * 64 + ((cell >> 7) & 7) * 8 + (cell >> 10)
        lane = cell & 127
        hot = one_hot(row, table_ref.shape[1])
        found = jnp.dot(table_ref[...], hot, preferred_element_type=F32)
        both = found[0:128] + found[128:256]
        rows = lax.broadcasted_iota(jnp.int32, both.shape, 0)
        got = jnp.sum(jnp.where(rows == lane, both, 0.0), axis=0, keepdims=True)
        val_s[pl.ds(2 * b, 1), :] = got[:, 0:128]
        val_s[pl.ds(2 * b + 1, 1), :] = got[:, 128:256]
        return carry

    lax.fori_loop(0, count // 2, gather, 0)
    elem_s[0:count, :] = key_ref[...] & 4095
    dir_s[0:count, :] = load_ref[...] >> 13

    lanes = lax.broadcasted_iota(jnp.int32, (8, 128), 1)
    subs = lax.broadcasted_iota(jnp.int32, (8, 128), 0)
    rank = subs * 128 + lanes

    def spread(o, carry):
        base = starts_ref[o]
        number = starts_ref[o + 1] - base
        first = base >> 7
        shift = base & 127
        valid = rank < number
        near = lanes < 128 - shift

        def window(ref):
            x = pltpu.roll(ref[pl.ds(first, 8), :], (128 - shift) & 127, 1)
            return jnp.where(near, x, pltpu.roll(x, 7, 0))

        value_ref[o] = jnp.where(valid, window(val_s), 0.0)[0:4]
        elem = window(elem_s)
        way = window(dir_s)
        where_ref[o] = jnp.where(subs < 4, elem, pltpu.roll(way, 4, 0))
        return carry

    lax.fori_loop(0, owners, spread, 0)


def facade_kernel(
    value_ref,
    where_ref,
    nodes_ref,
    grads_ref,
    area_ref,
    normal_ref,
    field_ref,
    force_ref,
    node_ref,
    acc_ref,
    hot_ref,
):
    owners = value_ref.shape[0]
    acc_ref[...] = jnp.zeros_like(acc_ref)

    def add(o, carry):
        value = value_ref[o]
        where = where_ref[o]

        def flat(x):
            return jnp.concatenate([x[r : r + 1] for r in range(x.shape[0])], axis=1)

        v = flat(value) * 2.0
        elem = flat(where[0:4])
        way = flat(where[4:8])
        group = elem >> 8
        low = elem & 255
        rows = lax.broadcasted_iota(jnp.int32, (16, v.shape[1]), 0)
        mine = rows == group
        parts = []
        for k in range(3):
            plus = functools.reduce(jnp.logical_or, [way == i for i in range(19) if SPEEDS[i][k] == 1])
            minus = functools.reduce(jnp.logical_or, [way == i for i in range(19) if SPEEDS[i][k] == -1])
            part = jnp.where(plus, v, jnp.where(minus, -v, 0.0))
            high = part.astype(BF16).astype(F32)
            parts.append(jnp.where(mine, high, 0.0))
            parts.append(jnp.where(mine, part - high, 0.0))
        left = jnp.concatenate(parts, axis=0).astype(BF16)
        hot = one_hot(low, 256)
        acc_ref[...] += lax.dot_general(
            left, hot, (((1,), (1,)), ((), ())), preferred_element_type=F32
        )
        return carry

    lax.fori_loop(0, owners, add, 0)
    forces = [acc_ref[32 * k : 32 * k + 16] + acc_ref[32 * k + 16 : 32 * k + 32] for k in range(3)]
    for h in range(16):
        force_ref[:, 256 * h : 256 * h + 256] = jnp.concatenate(
            [f[h : h + 1] for f in forces], axis=0
        )
    load = (
        normal_ref[0:1] * force_ref[0:1]
        + normal_ref[1:2] * force_ref[1:2]
        + normal_ref[2:3] * force_ref[2:3]
    ) / 3.0

    high, low = halves(field_ref[...])
    table = jnp.concatenate([high, low], axis=0)
    elements = nodes_ref.shape[1]
    values = []
    for j in range(3):
        node = nodes_ref[j : j + 1]
        pieces = []
        for b in range(elements // 512):
            n = node[:, 512 * b : 512 * b + 512]
            hot = one_hot(n & 127, 128)
            hot_ref[:, elements * j + 512 * b : elements * j + 512 * b + 512] = hot
            found = jnp.dot(table, hot, preferred_element_type=F32)
            both = found[0:32] + found[32:64]
            rows = lax.broadcasted_iota(jnp.int32, both.shape, 0)
            pieces.append(
                jnp.sum(jnp.where(rows == (n >> 7), both, 0.0), axis=0, keepdims=True)
            )
        values.append(jnp.concatenate(pieces, axis=1))
    g = [grads_ref[k : k + 1] for k in range(6)]
    slope_x = g[0] * values[0] + g[2] * values[1] + g[4] * values[2]
    slope_y = g[1] * values[0] + g[3] * values[1] + g[5] * values[2]
    area = area_ref[...]
    total = jnp.zeros((64, 128), F32)
    for j in range(3):
        term = load - area * (g[2 * j] * slope_x + g[2 * j + 1] * slope_y)
        node = nodes_ref[j : j + 1]
        for b in range(elements // 512):
            at = slice(512 * b, 512 * b + 512)
            part = term[:, at]
            rows = lax.broadcasted_iota(jnp.int32, (32, 512), 0)
            mine = rows == (node[:, at] >> 7)
            high = part.astype(BF16).astype(F32)
            left = jnp.concatenate(
                [jnp.where(mine, high, 0.0), jnp.where(mine, part - high, 0.0)], axis=0
            ).astype(BF16)
            hot = hot_ref[:, elements * j + 512 * b : elements * j + 512 * b + 512]
            total = total + lax.dot_general(
                left, hot, (((1,), (1,)), ((), ())), preferred_element_type=F32
            )
    node_ref[...] = total[0:32] + total[32:64]


def pass_kernel(post_ref, solid_ref, x_up_ref, x_down_ref, y_up_ref, y_down_ref, out_ref):
    is_solid = solid_ref[...] != 0
    rows, cols = is_solid.shape
    lanes = lax.broadcasted_iota(jnp.int32, (rows, cols), 1)
    lane = lax.broadcasted_iota(jnp.int32, (rows, 128), 1)
    height = lanes % NZ

    def marked(value, solid):
        return jnp.where(solid != 0.0, BLANK, value)

    for i in range(19):
        cx, cy, cz = SPEEDS[i]
        if i == 0:
            out_ref[0] = post_ref[0]
            continue
        value = jnp.where(is_solid, BLANK, post_ref[i])
        if cx == 1:
            q = X_UP.index(i)
            edge = marked(x_up_ref[q], x_up_ref[5])
            value = jnp.concatenate([edge, value[0 : rows - 1]], axis=0)
        elif cx == -1:
            q = X_DOWN.index(i)
            edge = marked(x_down_ref[q], x_down_ref[5])
            value = jnp.concatenate([value[1:rows], edge], axis=0)
        if cy == 1:
            q = Y_UP.index(i)
            edge = marked(y_up_ref[q, 1 - cx : 1 - cx + rows], y_up_ref[5, 1 - cx : 1 - cx + rows])
            value = pltpu.roll(value, NZ, 1)
            value = jnp.concatenate(
                [jnp.where(lane < NZ, edge, value[:, 0:128]), value[:, 128:]], axis=1
            )
        elif cy == -1:
            q = Y_DOWN.index(i)
            edge = marked(
                y_down_ref[q, 1 - cx : 1 - cx + rows], y_down_ref[5, 1 - cx : 1 - cx + rows]
            )
            value = pltpu.roll(value, cols - NZ, 1)
            value = jnp.concatenate(
                [value[:, : cols - 128], jnp.where(lane < NZ, value[:, cols - 128 :], edge)], axis=1
            )
        blocked = value == BLANK
        if cz != 0:
            value = pltpu.roll(value, 1 if cz == 1 else cols - 1, 1)
            blocked = (value == BLANK) | (height == (0 if cz == 1 else NZ - 1))
        value = jnp.where(blocked, post_ref[OPP[i]], value)
        out_ref[i] = jnp.where(is_solid, post_ref[i], value)


def call(kernel, out_shape, scratch=(), n_smem=0, n_vmem=0):
    return pl.pallas_call(
        kernel,
        out_shape=out_shape,
        in_specs=[pl.BlockSpec(memory_space=pltpu.SMEM)] * n_smem
        + [pl.BlockSpec(memory_space=pltpu.VMEM)] * n_vmem,
        out_specs=jax.tree.map(lambda _: pl.BlockSpec(memory_space=pltpu.VMEM), out_shape),
        scratch_shapes=list(scratch),
        compiler_params=pltpu.CompilerParams(vmem_limit_bytes=VMEM),
    )


def shift(array, axis, by):
    devices = lax.axis_size(axis)
    return lax.ppermute(array, axis, [(i, (i + by) % devices) for i in range(devices)])


def on_device(
    populations,
    solid,
    link_cell,
    link_dir,
    link_owner,
    link_elem,
    elem_nodes,
    elem_grads,
    elem_area,
    elem_normal,
    node_mass,
    displacement,
    velocity,
):
    everyone = ("gx", "gy")
    owners = lax.axis_size(everyone)
    elements = elem_nodes.shape[1]
    rows, cols = populations.shape[1:]
    rim = shift(displacement[:RIM], everyone, -1)
    owner = link_owner[:, 0]
    key, code = lax.sort(
        (owner * elements + link_elem, link_dir * (rows * cols) + link_cell), num_keys=1, is_stable=False
    )
    starts = jnp.sum(
        (owner[None, :] < jnp.arange(owners + 1, dtype=jnp.int32)[:, None]).astype(jnp.int32), axis=1
    )

    post, table = call(
        collide_kernel,
        (
            jax.ShapeDtypeStruct(populations.shape, F32),
            jax.ShapeDtypeStruct((256, 1152), BF16),
        ),
        n_vmem=2,
    )(populations, solid)

    flag = solid.astype(F32)[None]
    stacked = jnp.concatenate([post, flag], axis=0)
    up = jnp.stack([stacked[i, rows - 1 : rows] for i in X_UP + [19]])
    down = jnp.stack([stacked[i, 0:1] for i in X_DOWN + [19]])
    x_up = shift(up, "gx", 1)
    x_down = shift(down, "gx", -1)

    def taken(i, at):
        core = stacked[i, :, at]
        before = x_up[5 if i == 19 else X_UP.index(i), :, at] if i == 19 or i in X_UP else core[0:1]
        after = x_down[5 if i == 19 else X_DOWN.index(i), :, at] if i == 19 or i in X_DOWN else core[0:1]
        return jnp.concatenate([before, core, after], axis=0)

    y_up = shift(jnp.stack([taken(i, slice(cols - NZ, cols)) for i in Y_UP + [19]]), "gy", 1)
    y_down = shift(jnp.stack([taken(i, slice(0, NZ)) for i in Y_DOWN + [19]]), "gy", -1)
    y_up = jnp.pad(y_up, ((0, 0), (0, 0), (0, 128 - NZ)))
    y_down = jnp.pad(y_down, ((0, 0), (0, 0), (128 - NZ, 0)))

    value, where = call(
        links_kernel,
        (
            jax.ShapeDtypeStruct((owners, 4, 128), F32),
            jax.ShapeDtypeStruct((owners, 8, 128), jnp.int32),
        ),
        scratch=[
            pltpu.VMEM((136, 128), F32),
            pltpu.VMEM((136, 128), jnp.int32),
            pltpu.VMEM((136, 128), jnp.int32),
        ],
        n_smem=1,
        n_vmem=3,
    )(starts, key.reshape(-1, 128), code.reshape(-1, 128), table)

    where = lax.all_to_all(where, everyone, split_axis=0, concat_axis=0, tiled=True)
    value = lax.all_to_all(value, everyone, split_axis=0, concat_axis=0, tiled=True)

    field = jnp.concatenate(
        [displacement.reshape(-1, 128), rim.reshape(-1, 128), jnp.zeros((12, 128), F32)], axis=0
    )
    element_force, node_terms = call(
        facade_kernel,
        (
            jax.ShapeDtypeStruct((3, elements), F32),
            jax.ShapeDtypeStruct((32, 128), F32),
        ),
        scratch=[pltpu.VMEM((96, 256), F32), pltpu.VMEM((128, 3 * elements), BF16)],
        n_vmem=7,
    )(
        value,
        where,
        elem_nodes,
        elem_grads,
        elem_area.reshape(1, -1),
        elem_normal,
        field,
    )
    returned = shift(node_terms[16:20], everyone, 1)

    populations_out = call(
        pass_kernel, jax.ShapeDtypeStruct(populations.shape, F32), n_vmem=6
    )(post, solid, x_up, x_down, y_up, y_down)

    node_force = node_terms[0:16].at[0:4].add(returned).reshape(-1)
    velocity_out = velocity + time_step * node_force / node_mass
    displacement_out = displacement + time_step * velocity_out
    return (populations_out, element_force, displacement_out, velocity_out)


def solution(mesh):
    in_specs = (
        P(None, "gx", "gy"),
        P("gx", "gy"),
        P(("gx", "gy")),
        P(("gx", "gy")),
        P(("gx", "gy"), None),
        P(("gx", "gy")),
        P(None, ("gx", "gy")),
        P(None, ("gx", "gy")),
        P(("gx", "gy")),
        P(None, ("gx", "gy")),
        P(("gx", "gy")),
        P(("gx", "gy")),
        P(("gx", "gy")),
    )
    out_specs = (P(None, "gx", "gy"), P(None, ("gx", "gy")), P(("gx", "gy")), P(("gx", "gy")))
    return jax.shard_map(
        on_device, mesh=mesh, in_specs=in_specs, out_specs=out_specs, check_vma=False
    )
```

```python
import functools

import jax
import jax.numpy as jnp
from jax import lax
from jax.experimental import pallas as pl
from jax.experimental.pallas import tpu as pltpu
from jax.sharding import PartitionSpec as P

NZ = 64
RIM = 512
BLANK = -1e30

SPEEDS = [
    (0, 0, 0),
    (1, 0, 0),
    (-1, 0, 0),
    (0, 1, 0),
    (0, -1, 0),
    (0, 0, 1),
    (0, 0, -1),
    (1, 1, 0),
    (-1, -1, 0),
    (1, -1, 0),
    (-1, 1, 0),
    (1, 0, 1),
    (-1, 0, -1),
    (1, 0, -1),
    (-1, 0, 1),
    (0, 1, 1),
    (0, -1, -1),
    (0, 1, -1),
    (0, -1, 1),
]
WEIGHTS = [1.0 / 3.0] + [1.0 / 18.0] * 6 + [1.0 / 36.0] * 12
OPP = [0, 2, 1, 4, 3, 6, 5, 8, 7, 10, 9, 12, 11, 14, 13, 16, 15, 18, 17]
X_UP = [i for i in range(19) if SPEEDS[i][0] == 1]
X_DOWN = [i for i in range(19) if SPEEDS[i][0] == -1]
Y_UP = [i for i in range(19) if SPEEDS[i][1] == 1]
Y_DOWN = [i for i in range(19) if SPEEDS[i][1] == -1]
relax_time = 0.8
time_step = 0.5
VMEM = 48 * 1024 * 1024
F32 = jnp.float32
BF16 = jnp.bfloat16
MESH = pl.DeviceIdType.MESH
FIRST = 12
GROUP = 8


def halves(x):
    high = x.astype(BF16)
    return high, (x - high.astype(F32)).astype(BF16)


def signed_sum(terms):
    plus = [v for s, v in terms if s > 0]
    minus = [v for s, v in terms if s < 0]
    return functools.reduce(jnp.add, plus) - functools.reduce(jnp.add, minus)


def signed_sum_any(terms):
    total = None
    for s, v in terms:
        if total is None:
            total = v if s > 0 else -v
        else:
            total = total + v if s > 0 else total - v
    return total


def one_hot(index, size):
    rows = lax.broadcasted_iota(jnp.int16, (size, index.shape[1]), 0)
    return jnp.where(rows == index.astype(jnp.int16), jnp.ones((), BF16), jnp.zeros((), BF16))


def spread_rows(value_rows, index, size):
    rows = lax.broadcasted_iota(jnp.int16, (size, index.shape[1]), 0)
    mine = rows == index.astype(jnp.int16)
    return [jnp.where(mine, v, jnp.zeros((), BF16)) for v in value_rows]


def cut(starts_ref, o):
    lanes = lax.broadcasted_iota(jnp.int32, (8, 128), 1)
    subs = lax.broadcasted_iota(jnp.int32, (8, 128), 0)
    base = starts_ref[o]
    number = starts_ref[o + 1] - base
    first = base >> 7
    offset = base & 127
    near = lanes < 128 - offset

    def window(ref):
        x = pltpu.roll(ref[pl.ds(first, 8), :], (128 - offset) & 127, 1)
        return jnp.where(near, x, pltpu.roll(x, 7, 0))

    return window, subs * 128 + lanes < number, subs


def collide_kernel(
    starts_ref,
    popul_ref,
    solid_ref,
    key_ref,
    code_ref,
    post_ref,
    table_ref,
    where_ref,
    x_up_ref,
    x_down_ref,
    y_up_ref,
    y_down_ref,
    corner_ref,
    elem_s,
    dir_s,
):
    rows, cols = solid_ref.shape
    for t in range(cols // 128):
        at = pl.ds(128 * t, 128)
        f = [popul_ref[i, :, at] for i in range(19)]
        is_solid = solid_ref[:, at] != 0
        density = functools.reduce(jnp.add, f)
        inverse = 1.0 / density
        flow = [
            signed_sum([(SPEEDS[i][k], f[i]) for i in range(19) if SPEEDS[i][k] != 0]) * inverse
            for k in range(3)
        ]
        square = flow[0] * flow[0] + flow[1] * flow[1] + flow[2] * flow[2]
        rest = 1.0 - 1.5 * square
        keep = 1.0 - 1.0 / relax_time
        for i in range(19):
            if i != 0 and OPP[i] < i:
                continue
            scaled = (WEIGHTS[i] / relax_time) * density
            if i == 0:
                new = keep * f[0] + scaled * rest
                post_ref[0, :, at] = jnp.where(is_solid, f[0], new)
                continue
            along = signed_sum_any([(SPEEDS[i][k], flow[k]) for k in range(3) if SPEEDS[i][k] != 0])
            even = scaled * (rest + 4.5 * along * along)
            odd = scaled * (3.0 * along)
            j = OPP[i]
            post_ref[i, :, at] = jnp.where(is_solid, f[i], keep * f[i] + (even + odd))
            post_ref[j, :, at] = jnp.where(is_solid, f[j], keep * f[j] + (even - odd))
    for pair in range(9):
        block = jnp.concatenate(
            [
                post_ref[d, :, 128 * t : 128 * t + 128]
                for d in (1 + 2 * pair, 2 + 2 * pair)
                for t in range(cols // 128)
            ],
            axis=0,
        )
        high, low = halves(block.T)
        table_ref[0:128, 128 * pair : 128 * pair + 128] = high
        table_ref[128:256, 128 * pair : 128 * pair + 128] = low

    flag = solid_ref[...].astype(F32)
    for q in range(5):
        x_up_ref[q : q + 1] = post_ref[X_UP[q], rows - 1 : rows]
        x_down_ref[q : q + 1] = post_ref[X_DOWN[q], 0:1]
        y_up_ref[q] = post_ref[Y_UP[q], :, cols - 128 : cols]
        y_down_ref[q] = post_ref[Y_DOWN[q], :, 0:128]
    x_up_ref[5:6] = flag[rows - 1 : rows]
    x_down_ref[5:6] = flag[0:1]
    y_up_ref[5] = flag[:, cols - 128 : cols]
    y_down_ref[5] = flag[:, 0:128]
    for q in range(4):
        cx, cy, _ = SPEEDS[7 + q]
        row = slice(rows - 1, rows) if cx == 1 else slice(0, 1)
        lane = slice(cols - 128, cols) if cy == 1 else slice(0, 128)
        corner_ref[q, 0:1] = post_ref[7 + q, row, lane]
        corner_ref[q, 1:2] = flag[row, lane]

    count = key_ref.shape[0]
    elem_s[0:count, :] = key_ref[...] & 4095
    dir_s[0:count, :] = code_ref[...] >> 13

    def spread(o, carry):
        window, valid, subs = cut(starts_ref, o)
        elem = jnp.where(valid, window(elem_s), -1)
        where_ref[o] = jnp.where(subs < 4, elem, pltpu.roll(window(dir_s), 4, 0))
        return carry

    lax.fori_loop(0, where_ref.shape[0], spread, 0, unroll=8)


def exchange_kernel(
    starts_ref,
    code_ref,
    table_ref,
    where_ref,
    x_up_ref,
    x_down_ref,
    y_up_ref,
    y_down_ref,
    corner_ref,
    rim_ref,
    value_out,
    where_out,
    x_up_out,
    x_down_out,
    y_up_out,
    y_down_out,
    corner_out,
    rim_out,
    val_s,
    value_s,
    near_send,
    near_recv,
    where_send,
    where_recv,
    value_send,
    value_recv,
):
    count = code_ref.shape[0]
    gx, gy = lax.axis_index("gx"), lax.axis_index("gy")
    nx, ny = lax.axis_size("gx"), lax.axis_size("gy")
    owners = nx * ny
    me = gx * ny + gy

    def place(other):
        return (other // ny, lax.rem(other, ny))

    barrier = pltpu.get_barrier_semaphore()

    def greet(d, carry):
        other = lax.rem(me + d, owners)
        pl.semaphore_signal(barrier, inc=1, device_id=place(other), device_id_type=MESH)
        return carry

    lax.fori_loop(1, owners, greet, 0)

    span = 4

    def gather(b, carry):
        code = code_ref[pl.ds(pl.multiple_of(span * b, span), span), :]
        code = jnp.concatenate([code[r : r + 1] for r in range(span)], axis=1)
        cell = code & 8191
        row = ((code >> 13) - 1) * 64 + ((cell >> 7) & 7) * 8 + (cell >> 10)
        lane = cell & 127
        hot = one_hot(row, table_ref.shape[1])
        found = jnp.dot(table_ref[...], hot, preferred_element_type=F32)
        both = found[0:128] + found[128:256]
        rows = lax.broadcasted_iota(jnp.int32, both.shape, 0)
        got = jnp.sum(jnp.where(rows == lane, both, 0.0), axis=0, keepdims=True)
        for r in range(span):
            val_s[pl.ds(span * b + r, 1), :] = got[:, 128 * r : 128 * r + 128]
        return carry

    blocks = count // span
    val_s[count : count + 8, :] = jnp.zeros((8, 128), F32)
    lax.fori_loop(0, FIRST, gather, 0, unroll=4)
    pl.semaphore_wait(barrier, owners - 1)

    right, left = lax.rem(gx + 1, nx), lax.rem(gx + nx - 1, nx)
    above, below = lax.rem(gy + 1, ny), lax.rem(gy + ny - 1, ny)
    moves = [
        (x_up_ref, x_up_out, (right, gy)),
        (x_down_ref, x_down_out, (left, gy)),
        (y_up_ref, y_up_out, (gx, above)),
        (y_down_ref, y_down_out, (gx, below)),
        (corner_ref.at[0], corner_out.at[0], (right, above)),
        (corner_ref.at[1], corner_out.at[1], (left, below)),
        (corner_ref.at[2], corner_out.at[2], (right, below)),
        (corner_ref.at[3], corner_out.at[3], (left, above)),
        (rim_ref, rim_out, place(lax.rem(me + owners - 1, owners))),
    ]
    near = [
        pltpu.make_async_remote_copy(
            src_ref=src,
            dst_ref=dst,
            send_sem=near_send.at[q],
            recv_sem=near_recv.at[q],
            device_id=to,
            device_id_type=MESH,
        )
        for q, (src, dst, to) in enumerate(moves)
    ]
    for copy in near:
        copy.start()

    def send_where(d, carry):
        other = lax.rem(me + d, owners)
        pltpu.make_async_remote_copy(
            src_ref=where_ref.at[other],
            dst_ref=where_out.at[me],
            send_sem=where_send,
            recv_sem=where_recv,
            device_id=place(other),
            device_id_type=MESH,
        ).start()
        return carry

    lax.fori_loop(1, owners, send_where, 0)
    where_out[me] = where_ref[me]
    lax.fori_loop(FIRST, blocks, gather, 0, unroll=4)

    def fill(o):
        window, valid, _ = cut(starts_ref, o)
        return jnp.where(valid, window(val_s), 0.0)[0:4]

    value_out[me] = fill(me)

    def send_values(first, number):
        others = [lax.rem(me + first + r, owners) for r in range(number)]
        for other in others:
            value_s[other] = fill(other)
        for other in others:
            pltpu.make_async_remote_copy(
                src_ref=value_s.at[other],
                dst_ref=value_out.at[me],
                send_sem=value_send,
                recv_sem=value_recv,
                device_id=place(other),
                device_id_type=MESH,
            ).start()

    def send_group(g, carry):
        send_values(1 + GROUP * g, GROUP)
        return carry

    groups = (owners - 1) // GROUP
    lax.fori_loop(0, groups, send_group, 0)
    send_values(1 + GROUP * groups, owners - 1 - GROUP * groups)

    for copy in near:
        copy.wait()

    def whole(src, dst, send_sem, recv_sem):
        return pltpu.make_async_remote_copy(
            src_ref=src.at[pl.ds(0, owners - 1)],
            dst_ref=dst.at[pl.ds(0, owners - 1)],
            send_sem=send_sem,
            recv_sem=recv_sem,
            device_id=(right, gy),
            device_id_type=MESH,
        )

    whole(where_ref, where_out, where_send, where_recv).wait()
    whole(value_s, value_out, value_send, value_recv).wait()


def force_kernel(value_ref, where_ref, force_ref, acc_ref, count_v, count_s, list_s, sem):
    owners = value_ref.shape[0]
    span = 16
    groups, low_size = 32, 128
    acc_ref[...] = jnp.zeros_like(acc_ref)
    where = where_ref[...]
    subs = lax.broadcasted_iota(jnp.int32, where.shape, 1)
    held = jnp.sum(jnp.where((where >= 0) & (subs < 4), 1.0, 0.0).astype(F32), axis=1)
    got = lax.dot_general(
        jnp.ones((8, 128), BF16),
        held.astype(BF16),
        (((1,), (1,)), ((), ())),
        preferred_element_type=F32,
    )
    count_v[...] = got.astype(jnp.int32)
    copy = pltpu.make_async_copy(count_v, count_s, sem)
    copy.start()
    copy.wait()

    def fill(s, p):
        for r in range(4):
            list_s[p + r] = 4 * s + r
        return p + ((count_s[0, s] + 127) >> 7)

    total = lax.fori_loop(0, owners, fill, 0, unroll=4)
    for r in range(span):
        list_s[total + r] = 0

    def add(b, carry):
        values, elems, ways = [], [], []
        for r in range(span):
            i = span * b + r
            row = list_s[i]
            source, line = row >> 2, row & 3
            double = jnp.where(i < total, 2.0, 0.0)
            values.append(value_ref[source, pl.ds(line, 1), :] * double)
            elems.append(where_ref[source, pl.ds(line, 1), :])
            ways.append(where_ref[source, pl.ds(line + 4, 1), :])
        v = jnp.concatenate(values, axis=1)
        elem = jnp.concatenate(elems, axis=1)
        way = jnp.concatenate(ways, axis=1)
        bit = jnp.left_shift(jnp.ones_like(way), way)
        parts = []
        for k in range(3):
            plus = sum(1 << i for i in range(19) if SPEEDS[i][k] == 1)
            minus = sum(1 << i for i in range(19) if SPEEDS[i][k] == -1)
            part = jnp.where((bit & plus) != 0, v, jnp.where((bit & minus) != 0, -v, 0.0))
            parts.extend(halves(part))
        left = jnp.concatenate(spread_rows(parts, elem >> 7, groups), axis=0)
        hot = one_hot(elem & 127, low_size)
        acc_ref[...] += lax.dot_general(
            left, hot, (((1,), (1,)), ((), ())), preferred_element_type=F32
        )
        return carry

    lax.fori_loop(0, (total + span - 1) // span, add, 0)
    forces = [acc_ref[64 * k : 64 * k + 32] + acc_ref[64 * k + 32 : 64 * k + 64] for k in range(3)]
    for h in range(groups):
        force_ref[:, 128 * h : 128 * h + 128] = jnp.concatenate(
            [f[h : h + 1] for f in forces], axis=0
        )


def facade_kernel(
    force_ref,
    nodes_ref,
    grads_ref,
    area_ref,
    normal_ref,
    displacement_ref,
    rim_ref,
    velocity_ref,
    mass_ref,
    displacement_out,
    velocity_out,
    rim_s,
    return_s,
    send_sem,
    recv_sem,
):
    gx, gy = lax.axis_index("gx"), lax.axis_index("gy")
    nx, ny = lax.axis_size("gx"), lax.axis_size("gy")
    owners = nx * ny
    me = gx * ny + gy
    after, before = lax.rem(me + 1, owners), lax.rem(me + owners - 1, owners)
    barrier = pltpu.get_barrier_semaphore()
    for other in (after, before):
        pl.semaphore_signal(
            barrier, inc=1, device_id=(other // ny, lax.rem(other, ny)), device_id_type=MESH
        )

    load = (
        normal_ref[0:1] * force_ref[0:1]
        + normal_ref[1:2] * force_ref[1:2]
        + normal_ref[2:3] * force_ref[2:3]
    ) / 3.0
    field = jnp.concatenate([displacement_ref[...], rim_ref[...], jnp.zeros((12, 128), F32)], axis=0)
    table = jnp.concatenate(halves(field), axis=0)
    elements = nodes_ref.shape[1]
    values = []
    span = 1024
    for j in range(3):
        pieces = []
        for b in range(elements // span):
            n = nodes_ref[j : j + 1, span * b : span * b + span]
            found = jnp.dot(table, one_hot(n & 127, 128), preferred_element_type=F32)
            both = found[0:24] + found[32:56]
            rows = lax.broadcasted_iota(jnp.int32, both.shape, 0)
            pieces.append(jnp.sum(jnp.where(rows == (n >> 7), both, 0.0), axis=0, keepdims=True))
        values.append(jnp.concatenate(pieces, axis=1))
    g = [grads_ref[k : k + 1] for k in range(6)]
    slope_x = g[0] * values[0] + g[2] * values[1] + g[4] * values[2]
    slope_y = g[1] * values[0] + g[3] * values[1] + g[5] * values[2]
    area = area_ref[...]
    total = jnp.zeros((64, 128), F32)
    for j in range(3):
        term = load - area * (g[2 * j] * slope_x + g[2 * j + 1] * slope_y)
        for b in range(elements // span):
            at = slice(span * b, span * b + span)
            n = nodes_ref[j : j + 1, at]
            left = jnp.concatenate(spread_rows(halves(term[:, at]), n >> 7, 32), axis=0)
            total = total + lax.dot_general(
                left, one_hot(n & 127, 128), (((1,), (1,)), ((), ())), preferred_element_type=F32
            )
    node = total[0:32] + total[32:64]

    rim_s[...] = node[16:20]
    pl.semaphore_wait(barrier, 2)
    copy = pltpu.make_async_remote_copy(
        src_ref=rim_s,
        dst_ref=return_s,
        send_sem=send_sem,
        recv_sem=recv_sem,
        device_id=(after // ny, lax.rem(after, ny)),
        device_id_type=MESH,
    )
    copy.start()
    copy.wait()
    returned = jnp.concatenate([return_s[...], jnp.zeros((12, 128), F32)], axis=0)
    speed = velocity_ref[...] + time_step * (node[0:16] + returned) / mass_ref[...]
    velocity_out[...] = speed
    displacement_out[...] = displacement_ref[...] + time_step * speed


def pass_kernel(
    post_ref, solid_ref, x_up_ref, x_down_ref, y_up_ref, y_down_ref, corner_ref, out_ref
):
    is_solid = solid_ref[...] != 0
    rows, cols = is_solid.shape
    height = lax.broadcasted_iota(jnp.int32, (rows, cols), 1) % NZ
    lower = lax.broadcasted_iota(jnp.int32, (rows, 128), 1) < NZ

    def marked(value, solid):
        return jnp.where(solid != 0.0, BLANK, value)

    for i in range(19):
        cx, cy, cz = SPEEDS[i]
        if i == 0:
            out_ref[0] = post_ref[0]
            continue
        value = jnp.where(is_solid, BLANK, post_ref[i])

        def moved(core, first, last):
            if cx == 1:
                return jnp.concatenate([first(), core[0 : rows - 1]], axis=0)
            if cx == -1:
                return jnp.concatenate([core[1:rows], last()], axis=0)
            return core

        def x_edge(ref, names):
            q = names.index(i)
            return marked(ref[q : q + 1], ref[5:6])

        def corner():
            return marked(corner_ref[i - 7, 0:1], corner_ref[i - 7, 1:2])

        value = moved(value, lambda: x_edge(x_up_ref, X_UP), lambda: x_edge(x_down_ref, X_DOWN))
        if cy != 0:
            ref, names = (y_up_ref, Y_UP) if cy == 1 else (y_down_ref, Y_DOWN)
            edge = moved(marked(ref[names.index(i)], ref[5]), corner, corner)
            edge = pltpu.roll(edge, NZ, 1)
            value = pltpu.roll(value, NZ if cy == 1 else cols - NZ, 1)
            if cy == 1:
                value = jnp.concatenate(
                    [jnp.where(lower, edge, value[:, 0:128]), value[:, 128:]], axis=1
                )
            else:
                value = jnp.concatenate(
                    [value[:, : cols - 128], jnp.where(lower, value[:, cols - 128 :], edge)], axis=1
                )
        if cz != 0:
            value = pltpu.roll(value, 1 if cz == 1 else cols - 1, 1)
            blocked = (value == BLANK) | (height == (0 if cz == 1 else NZ - 1))
        else:
            blocked = value == BLANK
        value = jnp.where(blocked, post_ref[OPP[i]], value)
        out_ref[i] = jnp.where(is_solid, post_ref[i], value)


def call(kernel, out_shape, scratch=(), n_smem=0, n_vmem=0, **params):
    return pl.pallas_call(
        kernel,
        out_shape=out_shape,
        in_specs=[pl.BlockSpec(memory_space=pltpu.SMEM)] * n_smem
        + [pl.BlockSpec(memory_space=pltpu.VMEM)] * n_vmem,
        out_specs=jax.tree.map(lambda _: pl.BlockSpec(memory_space=pltpu.VMEM), out_shape),
        scratch_shapes=list(scratch),
        compiler_params=pltpu.CompilerParams(vmem_limit_bytes=VMEM, **params),
    )


def on_device(
    populations,
    solid,
    link_cell,
    link_dir,
    link_owner,
    link_elem,
    elem_nodes,
    elem_grads,
    elem_area,
    elem_normal,
    node_mass,
    displacement,
    velocity,
):
    owners = lax.axis_size(("gx", "gy"))
    elements = elem_nodes.shape[1]
    rows, cols = solid.shape
    owner = link_owner[:, 0]
    key, code = lax.sort(
        (owner * elements + link_elem, link_dir * (rows * cols) + link_cell), num_keys=1, is_stable=False
    )
    starts = jnp.sum(
        (owner[None, :] < jnp.arange(owners + 1, dtype=jnp.int32)[:, None]).astype(jnp.int32), axis=1
    )
    key, code = key.reshape(-1, 128), code.reshape(-1, 128)
    nodal = [x.reshape(-1, 128) for x in (displacement, velocity, node_mass)]

    def f32(*shape):
        return jax.ShapeDtypeStruct(shape, F32)

    halo_shapes = (f32(6, cols), f32(6, cols), f32(6, rows, 128), f32(6, rows, 128), f32(4, 2, 128))
    where_shape = jax.ShapeDtypeStruct((owners, 8, 128), jnp.int32)
    post, table, where, *halo = call(
        collide_kernel,
        (f32(*populations.shape), jax.ShapeDtypeStruct((256, 1152), BF16), where_shape, *halo_shapes),
        scratch=[pltpu.VMEM((136, 128), jnp.int32), pltpu.VMEM((136, 128), jnp.int32)],
        n_smem=1,
        n_vmem=4,
    )(starts, populations, solid, key, code)

    value, where, *halo, rim = call(
        exchange_kernel,
        (f32(owners, 4, 128), where_shape, *halo_shapes, f32(RIM // 128, 128)),
        scratch=[
            pltpu.VMEM((136, 128), F32),
            pltpu.VMEM((owners, 4, 128), F32),
            pltpu.SemaphoreType.DMA((9,)),
            pltpu.SemaphoreType.DMA((9,)),
            pltpu.SemaphoreType.DMA,
            pltpu.SemaphoreType.DMA,
            pltpu.SemaphoreType.DMA,
            pltpu.SemaphoreType.DMA,
        ],
        n_smem=1,
        n_vmem=9,
        collective_id=0,
        has_side_effects=True,
    )(starts, code, table, where, *halo, nodal[0][0 : RIM // 128])

    element_force = call(
        force_kernel,
        f32(3, elements),
        scratch=[
            pltpu.VMEM((192, 128), F32),
            pltpu.VMEM((8, 128), jnp.int32),
            pltpu.SMEM((8, 128), jnp.int32),
            pltpu.SMEM((544,), jnp.int32),
            pltpu.SemaphoreType.DMA,
        ],
        n_vmem=2,
    )(value, where)

    displacement_out, velocity_out = call(
        facade_kernel,
        (f32(16, 128), f32(16, 128)),
        scratch=[
            pltpu.VMEM((4, 128), F32),
            pltpu.VMEM((4, 128), F32),
            pltpu.SemaphoreType.DMA,
            pltpu.SemaphoreType.DMA,
        ],
        n_vmem=9,
        collective_id=1,
        has_side_effects=True,
    )(
        element_force,
        elem_nodes,
        elem_grads,
        elem_area.reshape(1, -1),
        elem_normal,
        nodal[0],
        rim,
        nodal[1],
        nodal[2],
    )

    populations_out = call(pass_kernel, f32(*populations.shape), n_vmem=7)(post, solid, *halo)
    return (populations_out, element_force, displacement_out.reshape(-1), velocity_out.reshape(-1))


def solution(mesh):
    in_specs = (
        P(None, "gx", "gy"),
        P("gx", "gy"),
        P(("gx", "gy")),
        P(("gx", "gy")),
        P(("gx", "gy"), None),
        P(("gx", "gy")),
        P(None, ("gx", "gy")),
        P(None, ("gx", "gy")),
        P(("gx", "gy")),
        P(None, ("gx", "gy")),
        P(("gx", "gy")),
        P(("gx", "gy")),
        P(("gx", "gy")),
    )
    out_specs = (P(None, "gx", "gy"), P(None, ("gx", "gy")), P(("gx", "gy")), P(("gx", "gy")))
    return jax.shard_map(
        on_device, mesh=mesh, in_specs=in_specs, out_specs=out_specs, check_vma=False
    )
```

```python
import functools

import jax
import jax.numpy as jnp
from jax import lax
from jax.experimental import pallas as pl
from jax.experimental.pallas import tpu as pltpu
from jax.sharding import PartitionSpec as P

NZ = 64
RIM = 512
BLANK = -1e30

SPEEDS = [
    (0, 0, 0),
    (1, 0, 0),
    (-1, 0, 0),
    (0, 1, 0),
    (0, -1, 0),
    (0, 0, 1),
    (0, 0, -1),
    (1, 1, 0),
    (-1, -1, 0),
    (1, -1, 0),
    (-1, 1, 0),
    (1, 0, 1),
    (-1, 0, -1),
    (1, 0, -1),
    (-1, 0, 1),
    (0, 1, 1),
    (0, -1, -1),
    (0, 1, -1),
    (0, -1, 1),
]
WEIGHTS = [1.0 / 3.0] + [1.0 / 18.0] * 6 + [1.0 / 36.0] * 12
OPP = [0, 2, 1, 4, 3, 6, 5, 8, 7, 10, 9, 12, 11, 14, 13, 16, 15, 18, 17]
X_UP = [i for i in range(19) if SPEEDS[i][0] == 1]
X_DOWN = [i for i in range(19) if SPEEDS[i][0] == -1]
Y_UP = [i for i in range(19) if SPEEDS[i][1] == 1]
Y_DOWN = [i for i in range(19) if SPEEDS[i][1] == -1]
relax_time = 0.8
time_step = 0.5
VMEM = 48 * 1024 * 1024
F32 = jnp.float32
BF16 = jnp.bfloat16
MESH = pl.DeviceIdType.MESH
FIRST = 4
SECOND = 12
GROUP = 8


def halves(x):
    high = x.astype(BF16)
    return high, (x - high.astype(F32)).astype(BF16)


def signed_sum(terms):
    plus = [v for s, v in terms if s > 0]
    minus = [v for s, v in terms if s < 0]
    return functools.reduce(jnp.add, plus) - functools.reduce(jnp.add, minus)


def signed_sum_any(terms):
    total = None
    for s, v in terms:
        if total is None:
            total = v if s > 0 else -v
        else:
            total = total + v if s > 0 else total - v
    return total


def one_hot(index, size):
    rows = lax.broadcasted_iota(jnp.int16, (size, index.shape[1]), 0)
    return jnp.where(rows == index.astype(jnp.int16), jnp.ones((), BF16), jnp.zeros((), BF16))


def spread_rows(value_rows, index, size):
    rows = lax.broadcasted_iota(jnp.int16, (size, index.shape[1]), 0)
    mine = rows == index.astype(jnp.int16)
    return [jnp.where(mine, v, jnp.zeros((), BF16)) for v in value_rows]


def cut(starts_ref, o):
    lanes = lax.broadcasted_iota(jnp.int32, (8, 128), 1)
    subs = lax.broadcasted_iota(jnp.int32, (8, 128), 0)
    base = starts_ref[0, o]
    number = starts_ref[1, o] - base
    first = base >> 7
    offset = base & 127
    near = lanes < 128 - offset

    def window(ref):
        x = pltpu.roll(ref[pl.ds(first, 8), :], (128 - offset) & 127, 1)
        return jnp.where(near, x, pltpu.roll(x, 7, 0))

    return window, subs * 128 + lanes < number, subs


def find_starts(owner):
    last = owner.T[127:128]
    lanes = lax.broadcasted_iota(jnp.int32, (1, 128), 1)
    previous = jnp.where(lanes == 0, -1.0, pltpu.roll(last, 1, 1))
    wanted = lax.broadcasted_iota(jnp.int32, (128, 128), 0).astype(F32)
    full = last < wanted
    split = jnp.where((last >= wanted) & (previous < wanted), 1.0, 0.0).astype(BF16)
    row = jnp.dot(split, (owner - 128.0).astype(BF16), preferred_element_type=F32)
    before = jnp.where(full, 128.0, 0.0) + jnp.where(row < wanted - 128.0, 1.0, 0.0)
    starts = lax.dot_general(
        jnp.ones((8, 128), BF16),
        before.astype(BF16),
        (((1,), (1,)), ((), ())),
        preferred_element_type=F32,
    ).astype(jnp.int32)
    lanes = lax.broadcasted_iota(jnp.int32, (8, 128), 1)
    subs = lax.broadcasted_iota(jnp.int32, (8, 128), 0)
    ends = jnp.where(lanes == 127, 128 * 128, pltpu.roll(starts, 127, 1))
    return jnp.where(subs == 0, starts, ends)


def collide_kernel(
    popul_hbm,
    solid_ref,
    key_ref,
    code_ref,
    displacement_ref,
    starts_ref,
    post_ref,
    table_ref,
    where_ref,
    x_up_ref,
    x_down_ref,
    y_up_ref,
    y_down_ref,
    corner_ref,
    field_ref,
    popul_ref,
    elem_s,
    dir_s,
    starts_v,
    popul_sem,
    starts_sem,
):
    rows, cols = solid_ref.shape
    bring = pltpu.make_async_copy(popul_hbm, popul_ref, popul_sem)
    bring.start()
    starts_v[...] = find_starts((key_ref[...] >> 12).astype(F32))
    copy = pltpu.make_async_copy(starts_v, starts_ref, starts_sem)
    copy.start()
    count = key_ref.shape[0]
    elem_s[0:count, :] = key_ref[...] & 4095
    dir_s[0:count, :] = code_ref[...] >> 13
    elem_s[count : count + 8, :] = jnp.zeros((8, 128), jnp.int32)
    dir_s[count : count + 8, :] = jnp.zeros((8, 128), jnp.int32)
    copy.wait()

    def spread(o, carry):
        window, valid, subs = cut(starts_ref, o)
        elem = jnp.where(valid, window(elem_s), -1)
        where_ref[lax.rem(o, ny), o // ny] = jnp.where(subs < 4, elem, pltpu.roll(window(dir_s), 4, 0))
        return carry

    ny, nx = where_ref.shape[:2]
    lax.fori_loop(0, nx * ny, spread, 0, unroll=8)
    field_ref[...] = displacement_ref[...]
    bring.wait()
    for t in range(cols // 128):
        at = pl.ds(128 * t, 128)
        f = [popul_ref[i, :, at] for i in range(19)]
        is_solid = solid_ref[:, at] != 0
        density = functools.reduce(jnp.add, f)
        inverse = 1.0 / density
        flow = [
            signed_sum([(SPEEDS[i][k], f[i]) for i in range(19) if SPEEDS[i][k] != 0]) * inverse
            for k in range(3)
        ]
        square = flow[0] * flow[0] + flow[1] * flow[1] + flow[2] * flow[2]
        rest = 1.0 - 1.5 * square
        keep = 1.0 - 1.0 / relax_time
        for i in range(19):
            if i != 0 and OPP[i] < i:
                continue
            scaled = (WEIGHTS[i] / relax_time) * density
            if i == 0:
                new = keep * f[0] + scaled * rest
                post_ref[0, :, at] = jnp.where(is_solid, f[0], new)
                continue
            along = signed_sum_any([(SPEEDS[i][k], flow[k]) for k in range(3) if SPEEDS[i][k] != 0])
            even = scaled * (rest + 4.5 * along * along)
            odd = scaled * (3.0 * along)
            j = OPP[i]
            post_ref[i, :, at] = jnp.where(is_solid, f[i], keep * f[i] + (even + odd))
            post_ref[j, :, at] = jnp.where(is_solid, f[j], keep * f[j] + (even - odd))
    for pair in range(9):
        block = jnp.concatenate(
            [
                post_ref[d, :, 128 * t : 128 * t + 128]
                for d in (1 + 2 * pair, 2 + 2 * pair)
                for t in range(cols // 128)
            ],
            axis=0,
        )
        high, low = halves(block.T)
        table_ref[0:128, 128 * pair : 128 * pair + 128] = high
        table_ref[128:256, 128 * pair : 128 * pair + 128] = low

    flag = solid_ref[...].astype(F32)
    for q in range(5):
        x_up_ref[q : q + 1] = post_ref[X_UP[q], rows - 1 : rows]
        x_down_ref[q : q + 1] = post_ref[X_DOWN[q], 0:1]
        y_up_ref[q] = post_ref[Y_UP[q], :, cols - 128 : cols]
        y_down_ref[q] = post_ref[Y_DOWN[q], :, 0:128]
    x_up_ref[5:6] = flag[rows - 1 : rows]
    x_down_ref[5:6] = flag[0:1]
    y_up_ref[5] = flag[:, cols - 128 : cols]
    y_down_ref[5] = flag[:, 0:128]
    for q in range(4):
        cx, cy, _ = SPEEDS[7 + q]
        row = slice(rows - 1, rows) if cx == 1 else slice(0, 1)
        lane = slice(cols - 128, cols) if cy == 1 else slice(0, 128)
        corner_ref[q, 0:1] = post_ref[7 + q, row, lane]
        corner_ref[q, 1:2] = flag[row, lane]


def exchange_kernel(
    starts_ref,
    code_ref,
    table_ref,
    where_ref,
    x_up_ref,
    x_down_ref,
    y_up_ref,
    y_down_ref,
    corner_ref,
    displacement_ref,
    nodes_ref,
    grads_ref,
    area_ref,
    value_out,
    where_out,
    x_up_out,
    x_down_out,
    y_up_out,
    y_down_out,
    corner_out,
    count_out,
    tension_out,
    rim_s,
    val_s,
    value_s,
    relay,
    all_in,
    near_send,
    near_recv,
    where_send,
    where_recv,
    value_send,
    value_recv,
):
    count = code_ref.shape[0]
    gx, gy = lax.axis_index("gx"), lax.axis_index("gy")
    nx, ny = lax.axis_size("gx"), lax.axis_size("gy")
    owners = nx * ny
    me = gx * ny + gy

    def place(other):
        return (other // ny, lax.rem(other, ny))

    barrier = pltpu.get_barrier_semaphore()

    row_peers = [(gx, lax.rem(gy + d, ny)) for d in range(1, ny)]
    column_peers = [(lax.rem(gx + d, nx), gy) for d in range(1, nx)]
    for other in row_peers + column_peers:
        pl.semaphore_signal(barrier, inc=1, device_id=other, device_id_type=MESH)

    span = 8

    def gather(b, carry):
        code = code_ref[pl.ds(pl.multiple_of(span * b, span), span), :]
        code = jnp.concatenate([code[r : r + 1] for r in range(span)], axis=1)
        cell = code & 8191
        row = ((code >> 13) - 1) * 64 + ((cell >> 7) & 7) * 8 + (cell >> 10)
        lane = cell & 127
        hot = one_hot(row, table_ref.shape[1])
        found = jnp.dot(table_ref[...], hot, preferred_element_type=F32)
        both = found[0:128] + found[128:256]
        rows = lax.broadcasted_iota(jnp.int32, both.shape, 0)
        got = jnp.sum(jnp.where(rows == lane, both, 0.0), axis=0, keepdims=True)
        for r in range(span):
            val_s[pl.ds(span * b + r, 1), :] = got[:, 128 * r : 128 * r + 128]
        return carry

    blocks = count // span
    val_s[count : count + 8, :] = jnp.zeros((8, 128), F32)

    lax.fori_loop(0, FIRST, gather, 0, unroll=2)
    pl.semaphore_wait(barrier, nx + ny - 2)
    for other in column_peers:
        pl.semaphore_signal(all_in, inc=1, device_id=other, device_id_type=MESH)

    right, left = lax.rem(gx + 1, nx), lax.rem(gx + nx - 1, nx)
    above, below = lax.rem(gy + 1, ny), lax.rem(gy + ny - 1, ny)
    moves = [
        (x_up_ref, x_up_out, (right, gy)),
        (x_down_ref, x_down_out, (left, gy)),
        (y_up_ref, y_up_out, (gx, above)),
        (y_down_ref, y_down_out, (gx, below)),
        (corner_ref.at[0], corner_out.at[0], (right, above)),
        (corner_ref.at[1], corner_out.at[1], (left, below)),
        (corner_ref.at[2], corner_out.at[2], (right, below)),
        (corner_ref.at[3], corner_out.at[3], (left, above)),
        (displacement_ref.at[0 : RIM // 128], rim_s, place(lax.rem(me + owners - 1, owners))),
    ]
    def remote(src, dst, send_sem, recv_sem, other):
        return pltpu.make_async_remote_copy(
            src_ref=src,
            dst_ref=dst,
            send_sem=send_sem,
            recv_sem=recv_sem,
            device_id=other,
            device_id_type=MESH,
        )

    for other in row_peers:
        remote(where_ref.at[other[1]], relay.at[gy], where_send.at[0], where_recv.at[0], other).start()
    relay[gy] = where_ref[gy]
    lax.fori_loop(FIRST, SECOND, gather, 0, unroll=2)
    remote(
        where_ref.at[pl.ds(0, ny - 1)],
        relay.at[pl.ds(0, ny - 1)],
        where_send.at[0],
        where_recv.at[0],
        (right, gy),
    ).wait()
    for other in column_peers:
        remote(
            relay.at[:, other[0]], where_out.at[gx], where_send.at[1], where_recv.at[1], other
        ).start()
    where_out[gx] = relay[:, gx]
    pl.semaphore_wait(all_in, nx - 1)
    near = [
        remote(src, dst, near_send.at[q], near_recv.at[q], to)
        for q, (src, dst, to) in enumerate(moves)
    ]
    for copy in near:
        copy.start()
    lax.fori_loop(SECOND, blocks, gather, 0, unroll=2)

    def fill(o):
        window, valid, _ = cut(starts_ref, o)
        return jnp.where(valid, window(val_s), 0.0)[0:4]

    value_out[me] = fill(me)

    def send_values(first, number):
        others = [lax.rem(me + first + r, owners) for r in range(number)]
        for other in others:
            value_s[other] = fill(other)
        for other in others:
            remote(
                value_s.at[other], value_out.at[me], value_send, value_recv, place(other)
            ).start()

    def send_group(g, carry):
        send_values(1 + GROUP * g, GROUP)
        return carry

    groups = (owners - 1) // GROUP
    lax.fori_loop(0, groups, send_group, 0)
    send_values(1 + GROUP * groups, owners - 1 - GROUP * groups)

    for copy in near:
        copy.wait()

    node_tension(displacement_ref, rim_s, nodes_ref, grads_ref, area_ref, tension_out)
    arrived = where_out.at[pl.ds(0, nx - 1)]
    remote(arrived, arrived, where_send.at[1], where_recv.at[1], (right, gy)).wait()
    where = where_out[...].reshape(owners, 8, 128)
    subs = lax.broadcasted_iota(jnp.int32, where.shape, 1)
    held = jnp.sum(jnp.where((where >= 0) & (subs < 4), 1.0, 0.0).astype(F32), axis=1)
    got = lax.dot_general(
        jnp.ones((8, 128), BF16),
        held.astype(BF16),
        (((1,), (1,)), ((), ())),
        preferred_element_type=F32,
    )
    count_out[...] = got.astype(jnp.int32)
    remote(
        value_s.at[pl.ds(0, owners - 1)],
        value_out.at[pl.ds(0, owners - 1)],
        value_send,
        value_recv,
        (right, gy),
    ).wait()


SPAN = 1024


def node_sums(nodes_ref, rows):
    total = jnp.zeros((64, 128), F32)
    for j in range(3):
        for b in range(nodes_ref.shape[1] // SPAN):
            at = slice(SPAN * b, SPAN * b + SPAN)
            n = nodes_ref[j : j + 1, at]
            left = jnp.concatenate(spread_rows(halves(rows[j][:, at]), n >> 7, 32), axis=0)
            total = total + lax.dot_general(
                left, one_hot(n & 127, 128), (((1,), (1,)), ((), ())), preferred_element_type=F32
            )
    return total[0:32] + total[32:64]


def node_tension(displacement_ref, rim_ref, nodes_ref, grads_ref, area_ref, tension_ref):
    field = jnp.concatenate([displacement_ref[...], rim_ref[...], jnp.zeros((12, 128), F32)], axis=0)
    table = jnp.concatenate(halves(field), axis=0)
    values = []
    for j in range(3):
        pieces = []
        for b in range(nodes_ref.shape[1] // SPAN):
            n = nodes_ref[j : j + 1, SPAN * b : SPAN * b + SPAN]
            found = jnp.dot(table, one_hot(n & 127, 128), preferred_element_type=F32)
            both = found[0:24] + found[32:56]
            rows = lax.broadcasted_iota(jnp.int32, both.shape, 0)
            pieces.append(jnp.sum(jnp.where(rows == (n >> 7), both, 0.0), axis=0, keepdims=True))
        values.append(jnp.concatenate(pieces, axis=1))
    g = [grads_ref[k : k + 1] for k in range(6)]
    area = area_ref[...]
    slope_x = area * (g[0] * values[0] + g[2] * values[1] + g[4] * values[2])
    slope_y = area * (g[1] * values[0] + g[3] * values[1] + g[5] * values[2])
    tension_ref[...] = node_sums(
        nodes_ref, [g[2 * j] * slope_x + g[2 * j + 1] * slope_y for j in range(3)]
    )


def force_kernel(count_s, value_ref, where_ref, normal_ref, force_ref, load_ref, acc_ref, list_s):
    owners = value_ref.shape[0]
    span = 64
    groups, low_size = 32, 128
    acc_ref[...] = jnp.zeros_like(acc_ref)

    def fill(s, p):
        for r in range(4):
            list_s[p + r] = 4 * s + r
        return p + ((count_s[0, s] + 127) >> 7)

    total = lax.fori_loop(0, owners, fill, 0, unroll=4)
    for r in range(span):
        list_s[total + r] = 0

    def add(b, carry):
        values, elems, ways = [], [], []
        for r in range(span):
            i = span * b + r
            row = list_s[i]
            source, line = row >> 2, row & 3
            double = jnp.where(i < total, 2.0, 0.0)
            values.append(value_ref[source, pl.ds(line, 1), :] * double)
            elems.append(where_ref[source, pl.ds(line, 1), :])
            ways.append(where_ref[source, pl.ds(line + 4, 1), :])
        v = jnp.concatenate(values, axis=1)
        elem = jnp.concatenate(elems, axis=1)
        way = jnp.concatenate(ways, axis=1)
        bit = jnp.left_shift(jnp.ones_like(way), way)
        parts = []
        for k in range(3):
            plus = sum(1 << i for i in range(19) if SPEEDS[i][k] == 1)
            minus = sum(1 << i for i in range(19) if SPEEDS[i][k] == -1)
            part = jnp.where((bit & plus) != 0, v, jnp.where((bit & minus) != 0, -v, 0.0))
            parts.extend(halves(part))
        left = jnp.concatenate(spread_rows(parts, elem >> 7, groups), axis=0)
        hot = one_hot(elem & 127, low_size)
        acc_ref[...] += lax.dot_general(
            left, hot, (((1,), (1,)), ((), ())), preferred_element_type=F32
        )
        return carry

    lax.fori_loop(0, (total + span - 1) // span, add, 0)
    forces = [acc_ref[64 * k : 64 * k + 32] + acc_ref[64 * k + 32 : 64 * k + 64] for k in range(3)]
    for h in range(groups):
        at = slice(128 * h, 128 * h + 128)
        lines = [f[h : h + 1] for f in forces]
        force_ref[:, at] = jnp.concatenate(lines, axis=0)
        load_ref[:, at] = sum(normal_ref[k : k + 1, at] * lines[k] for k in range(3)) / 3.0


def facade_kernel(load_ref, nodes_ref, tension_ref, node_out, returned_out, rim_s, return_s, send_sem, recv_sem):
    gx, gy = lax.axis_index("gx"), lax.axis_index("gy")
    nx, ny = lax.axis_size("gx"), lax.axis_size("gy")
    owners = nx * ny
    me = gx * ny + gy
    after, before = lax.rem(me + 1, owners), lax.rem(me + owners - 1, owners)
    barrier = pltpu.get_barrier_semaphore()
    for other in (after, before):
        pl.semaphore_signal(
            barrier, inc=1, device_id=(other // ny, lax.rem(other, ny)), device_id_type=MESH
        )
    node = node_sums(nodes_ref, [load_ref[...]] * 3) - tension_ref[...]
    rim_s[...] = node[16:20]
    pl.semaphore_wait(barrier, 2)
    copy = pltpu.make_async_remote_copy(
        src_ref=rim_s,
        dst_ref=return_s,
        send_sem=send_sem,
        recv_sem=recv_sem,
        device_id=(after // ny, lax.rem(after, ny)),
        device_id_type=MESH,
    )
    copy.start()
    node_out[...] = node[0:16]
    copy.wait()
    returned_out[...] = return_s[...]


def pass_kernel(
    post_ref,
    solid_ref,
    x_up_ref,
    x_down_ref,
    y_up_ref,
    y_down_ref,
    corner_ref,
    node_ref,
    returned_ref,
    displacement_ref,
    velocity_ref,
    mass_ref,
    out_ref,
    displacement_out,
    velocity_out,
):
    returned = jnp.concatenate([returned_ref[...], jnp.zeros((12, 128), F32)], axis=0)
    speed = velocity_ref[...] + time_step * (node_ref[...] + returned) / mass_ref[...]
    velocity_out[...] = speed
    displacement_out[...] = displacement_ref[...] + time_step * speed
    is_solid = solid_ref[...] != 0
    rows, cols = is_solid.shape
    height = lax.broadcasted_iota(jnp.int32, (rows, cols), 1) % NZ
    lower = lax.broadcasted_iota(jnp.int32, (rows, 128), 1) < NZ

    def marked(value, solid):
        return jnp.where(solid != 0.0, BLANK, value)

    for i in range(19):
        cx, cy, cz = SPEEDS[i]
        if i == 0:
            out_ref[0] = post_ref[0]
            continue
        value = jnp.where(is_solid, BLANK, post_ref[i])

        def moved(core, first, last):
            if cx == 1:
                return jnp.concatenate([first(), core[0 : rows - 1]], axis=0)
            if cx == -1:
                return jnp.concatenate([core[1:rows], last()], axis=0)
            return core

        def x_edge(ref, names):
            q = names.index(i)
            return marked(ref[q : q + 1], ref[5:6])

        def corner():
            return marked(corner_ref[i - 7, 0:1], corner_ref[i - 7, 1:2])

        value = moved(value, lambda: x_edge(x_up_ref, X_UP), lambda: x_edge(x_down_ref, X_DOWN))
        if cy != 0:
            ref, names = (y_up_ref, Y_UP) if cy == 1 else (y_down_ref, Y_DOWN)
            edge = moved(marked(ref[names.index(i)], ref[5]), corner, corner)
            edge = pltpu.roll(edge, NZ, 1)
            value = pltpu.roll(value, NZ if cy == 1 else cols - NZ, 1)
            if cy == 1:
                value = jnp.concatenate(
                    [jnp.where(lower, edge, value[:, 0:128]), value[:, 128:]], axis=1
                )
            else:
                value = jnp.concatenate(
                    [value[:, : cols - 128], jnp.where(lower, value[:, cols - 128 :], edge)], axis=1
                )
        if cz != 0:
            value = pltpu.roll(value, 1 if cz == 1 else cols - 1, 1)
            blocked = (value == BLANK) | (height == (0 if cz == 1 else NZ - 1))
        else:
            blocked = value == BLANK
        value = jnp.where(blocked, post_ref[OPP[i]], value)
        out_ref[i] = jnp.where(is_solid, post_ref[i], value)


def call(kernel, out_shape, scratch=(), n_vmem=0, n_smem=0, n_any=0, smem_out=0, **params):
    spaces = [pl.ANY] * n_any + [pltpu.SMEM] * n_smem + [pltpu.VMEM] * n_vmem
    outs = [pltpu.SMEM] * smem_out + [pltpu.VMEM] * (len(out_shape) - smem_out)
    return pl.pallas_call(
        kernel,
        out_shape=out_shape,
        in_specs=[pl.BlockSpec(memory_space=space) for space in spaces],
        out_specs=tuple(pl.BlockSpec(memory_space=space) for space in outs),
        scratch_shapes=list(scratch),
        compiler_params=pltpu.CompilerParams(vmem_limit_bytes=VMEM, **params),
    )


def on_device(
    populations,
    solid,
    link_cell,
    link_dir,
    link_owner,
    link_elem,
    elem_nodes,
    elem_grads,
    elem_area,
    elem_normal,
    node_mass,
    displacement,
    velocity,
):
    owners = lax.axis_size(("gx", "gy"))
    elements = elem_nodes.shape[1]
    rows, cols = solid.shape
    owner = lax.optimization_barrier(link_owner.reshape(-1))
    key, code = lax.sort(
        (owner * elements + link_elem, link_dir * (rows * cols) + link_cell), num_keys=1, is_stable=False
    )
    key, code = key.reshape(-1, 128), code.reshape(-1, 128)
    nodal = [x.reshape(-1, 128) for x in (displacement, velocity, node_mass)]

    def f32(*shape):
        return jax.ShapeDtypeStruct(shape, F32)

    halo_shapes = (f32(6, cols), f32(6, cols), f32(6, rows, 128), f32(6, rows, 128), f32(4, 2, 128))
    def i32(*shape):
        return jax.ShapeDtypeStruct(shape, jnp.int32)

    nx, ny = lax.axis_size("gx"), lax.axis_size("gy")
    where_shape = i32(ny, nx, 8, 128)
    starts, post, table, where, *halo, field = call(
        collide_kernel,
        (
            i32(8, 128),
            f32(*populations.shape),
            jax.ShapeDtypeStruct((256, 1152), BF16),
            where_shape,
            *halo_shapes,
            f32(16, 128),
        ),
        scratch=[
            pltpu.VMEM(populations.shape, F32),
            pltpu.VMEM((136, 128), jnp.int32),
            pltpu.VMEM((136, 128), jnp.int32),
            pltpu.VMEM((8, 128), jnp.int32),
            pltpu.SemaphoreType.DMA,
            pltpu.SemaphoreType.DMA,
        ],
        n_any=1,
        n_vmem=4,
        smem_out=1,
    )(populations, solid, key, code, nodal[0])

    value, where, *halo, counts, tension = call(
        exchange_kernel,
        (f32(owners, 4, 128), i32(nx, ny, 8, 128), *halo_shapes, i32(8, 128), f32(32, 128)),
        scratch=[
            pltpu.VMEM((RIM // 128, 128), F32),
            pltpu.VMEM((136, 128), F32),
            pltpu.VMEM((owners, 4, 128), F32),
            pltpu.VMEM(where_shape.shape, jnp.int32),
            pltpu.SemaphoreType.REGULAR,
            pltpu.SemaphoreType.DMA((9,)),
            pltpu.SemaphoreType.DMA((9,)),
            pltpu.SemaphoreType.DMA((2,)),
            pltpu.SemaphoreType.DMA((2,)),
            pltpu.SemaphoreType.DMA,
            pltpu.SemaphoreType.DMA,
        ],
        n_smem=1,
        n_vmem=12,
        collective_id=0,
        has_side_effects=True,
    )(starts, code, table, where, *halo, field, elem_nodes, elem_grads, elem_area.reshape(1, -1))

    element_force, load = call(
        force_kernel,
        (f32(3, elements), f32(1, elements)),
        scratch=[pltpu.VMEM((192, 128), F32), pltpu.SMEM((640,), jnp.int32)],
        n_smem=1,
        n_vmem=3,
    )(counts, value, where.reshape(owners, 8, 128), elem_normal)

    node, returned = call(
        facade_kernel,
        (f32(16, 128), f32(RIM // 128, 128)),
        scratch=[
            pltpu.VMEM((RIM // 128, 128), F32),
            pltpu.VMEM((RIM // 128, 128), F32),
            pltpu.SemaphoreType.DMA,
            pltpu.SemaphoreType.DMA,
        ],
        n_vmem=3,
        collective_id=1,
        has_side_effects=True,
    )(load, elem_nodes, tension)

    populations_out, displacement_out, velocity_out = call(
        pass_kernel,
        (f32(*populations.shape), f32(16, 128), f32(16, 128)),
        n_vmem=12,
    )(post, solid, *halo, node, returned, *nodal)
    return (populations_out, element_force, displacement_out.reshape(-1), velocity_out.reshape(-1))


def solution(mesh):
    in_specs = (
        P(None, "gx", "gy"),
        P("gx", "gy"),
        P(("gx", "gy")),
        P(("gx", "gy")),
        P(("gx", "gy"), None),
        P(("gx", "gy")),
        P(None, ("gx", "gy")),
        P(None, ("gx", "gy")),
        P(("gx", "gy")),
        P(None, ("gx", "gy")),
        P(("gx", "gy")),
        P(("gx", "gy")),
        P(("gx", "gy")),
    )
    out_specs = (P(None, "gx", "gy"), P(None, ("gx", "gy")), P(("gx", "gy")), P(("gx", "gy")))
    return jax.shard_map(
        on_device, mesh=mesh, in_specs=in_specs, out_specs=out_specs, check_vma=False
    )
```

```python
import functools

import jax
import jax.numpy as jnp
from jax import lax
from jax.experimental import pallas as pl
from jax.experimental.pallas import tpu as pltpu
from jax.sharding import PartitionSpec as P

NZ = 64
RIM = 512
BLANK = -1e30

SPEEDS = [
    (0, 0, 0),
    (1, 0, 0),
    (-1, 0, 0),
    (0, 1, 0),
    (0, -1, 0),
    (0, 0, 1),
    (0, 0, -1),
    (1, 1, 0),
    (-1, -1, 0),
    (1, -1, 0),
    (-1, 1, 0),
    (1, 0, 1),
    (-1, 0, -1),
    (1, 0, -1),
    (-1, 0, 1),
    (0, 1, 1),
    (0, -1, -1),
    (0, 1, -1),
    (0, -1, 1),
]
WEIGHTS = [1.0 / 3.0] + [1.0 / 18.0] * 6 + [1.0 / 36.0] * 12
OPP = [0, 2, 1, 4, 3, 6, 5, 8, 7, 10, 9, 12, 11, 14, 13, 16, 15, 18, 17]
X_UP = [i for i in range(19) if SPEEDS[i][0] == 1]
X_DOWN = [i for i in range(19) if SPEEDS[i][0] == -1]
Y_UP = [i for i in range(19) if SPEEDS[i][1] == 1]
Y_DOWN = [i for i in range(19) if SPEEDS[i][1] == -1]
relax_time = 0.8
time_step = 0.5
VMEM = 48 * 1024 * 1024
F32 = jnp.float32
BF16 = jnp.bfloat16
MESH = pl.DeviceIdType.MESH
FIRST = 4
SECOND = 12
GROUP = 8


def halves(x):
    high = x.astype(BF16)
    return high, (x - high.astype(F32)).astype(BF16)


def signed_sum(terms):
    plus = [v for s, v in terms if s > 0]
    minus = [v for s, v in terms if s < 0]
    return functools.reduce(jnp.add, plus) - functools.reduce(jnp.add, minus)


def signed_sum_any(terms):
    total = None
    for s, v in terms:
        if total is None:
            total = v if s > 0 else -v
        else:
            total = total + v if s > 0 else total - v
    return total


def one_hot(index, size):
    rows = lax.broadcasted_iota(jnp.int16, (size, index.shape[1]), 0)
    return jnp.where(rows == index.astype(jnp.int16), jnp.ones((), BF16), jnp.zeros((), BF16))


def spread_rows(value_rows, index, size):
    rows = lax.broadcasted_iota(jnp.int16, (size, index.shape[1]), 0)
    mine = rows == index.astype(jnp.int16)
    return [jnp.where(mine, v, jnp.zeros((), BF16)) for v in value_rows]


def cut(starts_ref, o):
    lanes = lax.broadcasted_iota(jnp.int32, (8, 128), 1)
    subs = lax.broadcasted_iota(jnp.int32, (8, 128), 0)
    base = starts_ref[0, o]
    number = starts_ref[1, o] - base
    first = base >> 7
    offset = base & 127
    near = lanes < 128 - offset

    def window(ref):
        x = pltpu.roll(ref[pl.ds(first, 8), :], (128 - offset) & 127, 1)
        return jnp.where(near, x, pltpu.roll(x, 7, 0))

    return window, subs * 128 + lanes < number, subs


def find_starts(owner):
    last = owner.T[127:128]
    lanes = lax.broadcasted_iota(jnp.int32, (1, 128), 1)
    previous = jnp.where(lanes == 0, -1.0, pltpu.roll(last, 1, 1))
    wanted = lax.broadcasted_iota(jnp.int32, (128, 128), 0).astype(F32)
    full = last < wanted
    split = jnp.where((last >= wanted) & (previous < wanted), 1.0, 0.0).astype(BF16)
    row = jnp.dot(split, (owner - 128.0).astype(BF16), preferred_element_type=F32)
    before = jnp.where(full, 128.0, 0.0) + jnp.where(row < wanted - 128.0, 1.0, 0.0)
    starts = lax.dot_general(
        jnp.ones((8, 128), BF16),
        before.astype(BF16),
        (((1,), (1,)), ((), ())),
        preferred_element_type=F32,
    ).astype(jnp.int32)
    lanes = lax.broadcasted_iota(jnp.int32, (8, 128), 1)
    subs = lax.broadcasted_iota(jnp.int32, (8, 128), 0)
    ends = jnp.where(lanes == 127, 128 * 128, pltpu.roll(starts, 127, 1))
    return jnp.where(subs == 0, starts, ends)


def cut_kernel(key_ref, code_ref, starts_ref, elem_ref, dir_ref, elem_s, dir_s, starts_v, sem):
    starts_v[...] = find_starts((key_ref[...] >> 12).astype(F32))
    copy = pltpu.make_async_copy(starts_v, starts_ref, sem)
    copy.start()
    count = key_ref.shape[0]
    elem_s[0:count, :] = key_ref[...] & 4095
    dir_s[0:count, :] = code_ref[...] >> 13
    elem_s[count : count + 8, :] = jnp.zeros((8, 128), jnp.int32)
    dir_s[count : count + 8, :] = jnp.zeros((8, 128), jnp.int32)
    copy.wait()
    ny, nx = elem_ref.shape[:2]

    def spread(o, carry):
        window, valid, _ = cut(starts_ref, o)
        x, y = o // ny, lax.rem(o, ny)
        elem_ref[y, x] = jnp.where(valid, window(elem_s), -1)[0:4]
        dir_ref[x, y] = window(dir_s)[0:4]
        return carry

    lax.fori_loop(0, nx * ny, spread, 0, unroll=8)


def collide_kernel(
    popul_ref,
    solid_ref,
    displacement_ref,
    area_ref,
    starts_ref,
    post_ref,
    table_ref,
    x_up_ref,
    x_down_ref,
    y_up_ref,
    y_down_ref,
    corner_ref,
    field_out,
    area_out,
    starts_out,
):
    rows, cols = solid_ref.shape
    field_out[...] = displacement_ref[...]
    area_out[...] = area_ref[...]
    starts_out[...] = starts_ref[...]
    for t in range(cols // 128):
        at = pl.ds(128 * t, 128)
        f = [popul_ref[i, :, at] for i in range(19)]
        is_solid = solid_ref[:, at] != 0
        density = functools.reduce(jnp.add, f)
        inverse = 1.0 / density
        flow = [
            signed_sum([(SPEEDS[i][k], f[i]) for i in range(19) if SPEEDS[i][k] != 0]) * inverse
            for k in range(3)
        ]
        square = flow[0] * flow[0] + flow[1] * flow[1] + flow[2] * flow[2]
        rest = 1.0 - 1.5 * square
        keep = 1.0 - 1.0 / relax_time
        for i in range(19):
            if i != 0 and OPP[i] < i:
                continue
            scaled = (WEIGHTS[i] / relax_time) * density
            if i == 0:
                new = keep * f[0] + scaled * rest
                post_ref[0, :, at] = jnp.where(is_solid, f[0], new)
                continue
            along = signed_sum_any([(SPEEDS[i][k], flow[k]) for k in range(3) if SPEEDS[i][k] != 0])
            even = scaled * (rest + 4.5 * along * along)
            odd = scaled * (3.0 * along)
            j = OPP[i]
            post_ref[i, :, at] = jnp.where(is_solid, f[i], keep * f[i] + (even + odd))
            post_ref[j, :, at] = jnp.where(is_solid, f[j], keep * f[j] + (even - odd))
    for pair in range(9):
        block = jnp.concatenate(
            [
                post_ref[d, :, 128 * t : 128 * t + 128]
                for d in (1 + 2 * pair, 2 + 2 * pair)
                for t in range(cols // 128)
            ],
            axis=0,
        )
        high, low = halves(block.T)
        table_ref[0:128, 128 * pair : 128 * pair + 128] = high
        table_ref[128:256, 128 * pair : 128 * pair + 128] = low

    flag = solid_ref[...].astype(F32)
    for q in range(5):
        x_up_ref[q : q + 1] = post_ref[X_UP[q], rows - 1 : rows]
        x_down_ref[q : q + 1] = post_ref[X_DOWN[q], 0:1]
        y_up_ref[q] = post_ref[Y_UP[q], :, cols - 128 : cols]
        y_down_ref[q] = post_ref[Y_DOWN[q], :, 0:128]
    x_up_ref[5:6] = flag[rows - 1 : rows]
    x_down_ref[5:6] = flag[0:1]
    y_up_ref[5] = flag[:, cols - 128 : cols]
    y_down_ref[5] = flag[:, 0:128]
    for q in range(4):
        cx, cy, _ = SPEEDS[7 + q]
        row = slice(rows - 1, rows) if cx == 1 else slice(0, 1)
        lane = slice(cols - 128, cols) if cy == 1 else slice(0, 128)
        corner_ref[q, 0:1] = post_ref[7 + q, row, lane]
        corner_ref[q, 1:2] = flag[row, lane]


def exchange_kernel(
    starts_ref,
    code_ref,
    table_ref,
    elem_ref,
    dir_ref,
    x_up_ref,
    x_down_ref,
    y_up_ref,
    y_down_ref,
    corner_ref,
    displacement_ref,
    nodes_ref,
    grads_ref,
    area_ref,
    value_out,
    elem_out,
    dir_out,
    x_up_out,
    x_down_out,
    y_up_out,
    y_down_out,
    corner_out,
    count_out,
    tension_out,
    rim_s,
    val_s,
    value_s,
    elem_relay,
    dir_relay,
    all_in,
    near_send,
    near_recv,
    elem_send,
    elem_recv,
    dir_send,
    dir_recv,
    value_send,
    value_recv,
):
    count = code_ref.shape[0]
    gx, gy = lax.axis_index("gx"), lax.axis_index("gy")
    nx, ny = lax.axis_size("gx"), lax.axis_size("gy")
    owners = nx * ny
    me = gx * ny + gy

    def place(other):
        return (other // ny, lax.rem(other, ny))

    barrier = pltpu.get_barrier_semaphore()

    row_peers = [(gx, lax.rem(gy + d, ny)) for d in range(1, ny)]
    column_peers = [(lax.rem(gx + d, nx), gy) for d in range(1, nx)]
    for other in row_peers + column_peers:
        pl.semaphore_signal(barrier, inc=1, device_id=other, device_id_type=MESH)

    span = 8

    def gather(b, carry):
        code = code_ref[pl.ds(pl.multiple_of(span * b, span), span), :]
        code = jnp.concatenate([code[r : r + 1] for r in range(span)], axis=1)
        cell = code & 8191
        row = ((code >> 13) - 1) * 64 + ((cell >> 7) & 7) * 8 + (cell >> 10)
        lane = cell & 127
        hot = one_hot(row, table_ref.shape[1])
        found = jnp.dot(table_ref[...], hot, preferred_element_type=F32)
        both = found[0:128] + found[128:256]
        rows = lax.broadcasted_iota(jnp.int32, both.shape, 0)
        got = jnp.sum(jnp.where(rows == lane, both, 0.0), axis=0, keepdims=True)
        for r in range(span):
            val_s[pl.ds(span * b + r, 1), :] = got[:, 128 * r : 128 * r + 128]
        return carry

    blocks = count // span
    val_s[count : count + 8, :] = jnp.zeros((8, 128), F32)

    lax.fori_loop(0, FIRST, gather, 0, unroll=2)
    pl.semaphore_wait(barrier, nx + ny - 2)
    for other in column_peers:
        pl.semaphore_signal(all_in, inc=1, device_id=other, device_id_type=MESH)

    right, left = lax.rem(gx + 1, nx), lax.rem(gx + nx - 1, nx)
    above, below = lax.rem(gy + 1, ny), lax.rem(gy + ny - 1, ny)
    moves = [
        (x_up_ref, x_up_out, (right, gy)),
        (x_down_ref, x_down_out, (left, gy)),
        (y_up_ref, y_up_out, (gx, above)),
        (y_down_ref, y_down_out, (gx, below)),
        (corner_ref.at[0], corner_out.at[0], (right, above)),
        (corner_ref.at[1], corner_out.at[1], (left, below)),
        (corner_ref.at[2], corner_out.at[2], (right, below)),
        (corner_ref.at[3], corner_out.at[3], (left, above)),
        (displacement_ref.at[0 : RIM // 128], rim_s, place(lax.rem(me + owners - 1, owners))),
    ]
    def remote(src, dst, send_sem, recv_sem, other):
        return pltpu.make_async_remote_copy(
            src_ref=src,
            dst_ref=dst,
            send_sem=send_sem,
            recv_sem=recv_sem,
            device_id=other,
            device_id_type=MESH,
        )

    def settle(buffer, number, send_sem, recv_sem):
        part = buffer.at[pl.ds(0, number)]
        remote(part, part, send_sem, recv_sem, (right, gy)).wait()

    for other in row_peers:
        remote(elem_ref.at[other[1]], elem_relay.at[gy], elem_send.at[0], elem_recv.at[0], other).start()
    for other in column_peers:
        remote(dir_ref.at[other[0]], dir_relay.at[gx], dir_send.at[0], dir_recv.at[0], other).start()
    elem_relay[gy] = elem_ref[gy]
    dir_relay[gx] = dir_ref[gx]
    lax.fori_loop(FIRST, SECOND, gather, 0, unroll=2)
    settle(elem_relay, ny - 1, elem_send.at[0], elem_recv.at[0])
    settle(dir_relay, nx - 1, dir_send.at[0], dir_recv.at[0])
    for other in column_peers:
        remote(
            elem_relay.at[:, other[0]], elem_out.at[gx], elem_send.at[1], elem_recv.at[1], other
        ).start()
    for other in row_peers:
        remote(
            dir_relay.at[:, other[1]], dir_out.at[gy], dir_send.at[1], dir_recv.at[1], other
        ).start()
    elem_out[gx] = elem_relay[:, gx]
    dir_out[gy] = dir_relay[:, gy]
    pl.semaphore_wait(all_in, nx - 1)
    near = [
        remote(src, dst, near_send.at[q], near_recv.at[q], to)
        for q, (src, dst, to) in enumerate(moves)
    ]
    for copy in near:
        copy.start()
    lax.fori_loop(SECOND, blocks, gather, 0, unroll=2)

    def fill(o):
        window, valid, _ = cut(starts_ref, o)
        return jnp.where(valid, window(val_s), 0.0)[0:4]

    value_out[me] = fill(me)

    def send_values(first, number):
        others = [lax.rem(me + first + r, owners) for r in range(number)]
        for other in others:
            value_s[other] = fill(other)
        for other in others:
            remote(
                value_s.at[other], value_out.at[me], value_send, value_recv, place(other)
            ).start()

    def send_group(g, carry):
        send_values(1 + GROUP * g, GROUP)
        return carry

    groups = (owners - 1) // GROUP
    lax.fori_loop(0, groups, send_group, 0)
    send_values(1 + GROUP * groups, owners - 1 - GROUP * groups)

    for copy in near:
        copy.wait()

    node_tension(displacement_ref, rim_s, nodes_ref, grads_ref, area_ref, tension_out)
    settle(elem_out, nx - 1, elem_send.at[1], elem_recv.at[1])
    settle(dir_out, ny - 1, dir_send.at[1], dir_recv.at[1])
    elem = elem_out[...].reshape(owners, 4, 128)
    held = jnp.sum(jnp.where(elem >= 0, 1.0, 0.0).astype(F32), axis=1)
    got = lax.dot_general(
        jnp.ones((8, 128), BF16),
        held.astype(BF16),
        (((1,), (1,)), ((), ())),
        preferred_element_type=F32,
    )
    count_out[...] = got.astype(jnp.int32)
    remote(
        value_s.at[pl.ds(0, owners - 1)],
        value_out.at[pl.ds(0, owners - 1)],
        value_send,
        value_recv,
        (right, gy),
    ).wait()


SPAN = 1024


def node_sums(nodes_ref, rows):
    total = jnp.zeros((64, 128), F32)
    for j in range(3):
        for b in range(nodes_ref.shape[1] // SPAN):
            at = slice(SPAN * b, SPAN * b + SPAN)
            n = nodes_ref[j : j + 1, at]
            left = jnp.concatenate(spread_rows(halves(rows[j][:, at]), n >> 7, 32), axis=0)
            total = total + lax.dot_general(
                left, one_hot(n & 127, 128), (((1,), (1,)), ((), ())), preferred_element_type=F32
            )
    return total[0:32] + total[32:64]


def node_tension(displacement_ref, rim_ref, nodes_ref, grads_ref, area_ref, tension_ref):
    field = jnp.concatenate([displacement_ref[...], rim_ref[...], jnp.zeros((12, 128), F32)], axis=0)
    table = jnp.concatenate(halves(field), axis=0)
    values = []
    for j in range(3):
        pieces = []
        for b in range(nodes_ref.shape[1] // SPAN):
            n = nodes_ref[j : j + 1, SPAN * b : SPAN * b + SPAN]
            found = jnp.dot(table, one_hot(n & 127, 128), preferred_element_type=F32)
            both = found[0:24] + found[32:56]
            rows = lax.broadcasted_iota(jnp.int32, both.shape, 0)
            pieces.append(jnp.sum(jnp.where(rows == (n >> 7), both, 0.0), axis=0, keepdims=True))
        values.append(jnp.concatenate(pieces, axis=1))
    g = [grads_ref[k : k + 1] for k in range(6)]
    area = area_ref[...]
    slope_x = area * (g[0] * values[0] + g[2] * values[1] + g[4] * values[2])
    slope_y = area * (g[1] * values[0] + g[3] * values[1] + g[5] * values[2])
    tension_ref[...] = node_sums(
        nodes_ref, [g[2 * j] * slope_x + g[2 * j + 1] * slope_y for j in range(3)]
    )


def force_kernel(
    count_s, value_ref, elem_ref, dir_ref, normal_ref, force_ref, load_ref, acc_ref, list_s
):
    owners = value_ref.shape[0]
    span = 128
    groups, low_size = 32, 128
    nx, ny = lax.axis_size("gx"), lax.axis_size("gy")
    acc_ref[...] = jnp.zeros_like(acc_ref)

    def fill(s, p):
        for r in range(4):
            list_s[p + r] = 4 * s + r
        return p + ((count_s[0, s] + 127) >> 7)

    total = lax.fori_loop(0, owners, fill, 0, unroll=4)
    for r in range(span):
        list_s[total + r] = 0

    def add(b, carry):
        values, elems, ways = [], [], []
        for r in range(span):
            i = span * b + r
            row = list_s[i]
            source, line = row >> 2, row & 3
            double = jnp.where(i < total, 2.0, 0.0)
            values.append(value_ref[source, pl.ds(line, 1), :] * double)
            elems.append(elem_ref[source, pl.ds(line, 1), :])
            ways.append(dir_ref[lax.rem(source, ny) * nx + source // ny, pl.ds(line, 1), :])
        v = jnp.concatenate(values, axis=1)
        elem = jnp.concatenate(elems, axis=1)
        way = jnp.concatenate(ways, axis=1)
        bit = jnp.left_shift(jnp.ones_like(way), way)
        parts = []
        for k in range(3):
            plus = sum(1 << i for i in range(19) if SPEEDS[i][k] == 1)
            minus = sum(1 << i for i in range(19) if SPEEDS[i][k] == -1)
            part = jnp.where((bit & plus) != 0, v, jnp.where((bit & minus) != 0, -v, 0.0))
            parts.extend(halves(part))
        left = jnp.concatenate(spread_rows(parts, elem >> 7, groups), axis=0)
        hot = one_hot(elem & 127, low_size)
        acc_ref[...] += lax.dot_general(
            left, hot, (((1,), (1,)), ((), ())), preferred_element_type=F32
        )
        return carry

    lax.fori_loop(0, (total + span - 1) // span, add, 0)
    forces = [acc_ref[64 * k : 64 * k + 32] + acc_ref[64 * k + 32 : 64 * k + 64] for k in range(3)]
    for h in range(groups):
        at = slice(128 * h, 128 * h + 128)
        lines = [f[h : h + 1] for f in forces]
        force_ref[:, at] = jnp.concatenate(lines, axis=0)
        load_ref[:, at] = sum(normal_ref[k : k + 1, at] * lines[k] for k in range(3)) / 3.0


def facade_kernel(load_ref, nodes_ref, tension_ref, node_out, returned_out, rim_s, return_s, send_sem, recv_sem):
    gx, gy = lax.axis_index("gx"), lax.axis_index("gy")
    nx, ny = lax.axis_size("gx"), lax.axis_size("gy")
    owners = nx * ny
    me = gx * ny + gy
    after, before = lax.rem(me + 1, owners), lax.rem(me + owners - 1, owners)
    barrier = pltpu.get_barrier_semaphore()
    for other in (after, before):
        pl.semaphore_signal(
            barrier, inc=1, device_id=(other // ny, lax.rem(other, ny)), device_id_type=MESH
        )
    node = node_sums(nodes_ref, [load_ref[...]] * 3) - tension_ref[...]
    rim_s[...] = node[16:20]
    pl.semaphore_wait(barrier, 2)
    copy = pltpu.make_async_remote_copy(
        src_ref=rim_s,
        dst_ref=return_s,
        send_sem=send_sem,
        recv_sem=recv_sem,
        device_id=(after // ny, lax.rem(after, ny)),
        device_id_type=MESH,
    )
    copy.start()
    node_out[...] = node[0:16]
    copy.wait()
    returned_out[...] = return_s[...]


def pass_kernel(
    post_ref,
    solid_ref,
    x_up_ref,
    x_down_ref,
    y_up_ref,
    y_down_ref,
    corner_ref,
    node_ref,
    returned_ref,
    displacement_ref,
    velocity_ref,
    mass_ref,
    out_ref,
    displacement_out,
    velocity_out,
):
    returned = jnp.concatenate([returned_ref[...], jnp.zeros((12, 128), F32)], axis=0)
    speed = velocity_ref[...] + time_step * (node_ref[...] + returned) / mass_ref[...]
    velocity_out[...] = speed
    displacement_out[...] = displacement_ref[...] + time_step * speed
    is_solid = solid_ref[...] != 0
    rows, cols = is_solid.shape
    height = lax.broadcasted_iota(jnp.int32, (rows, cols), 1) % NZ
    lower = lax.broadcasted_iota(jnp.int32, (rows, 128), 1) < NZ

    def marked(value, solid):
        return jnp.where(solid != 0.0, BLANK, value)

    for i in range(19):
        cx, cy, cz = SPEEDS[i]
        if i == 0:
            out_ref[0] = post_ref[0]
            continue
        value = jnp.where(is_solid, BLANK, post_ref[i])

        def moved(core, first, last):
            if cx == 1:
                return jnp.concatenate([first(), core[0 : rows - 1]], axis=0)
            if cx == -1:
                return jnp.concatenate([core[1:rows], last()], axis=0)
            return core

        def x_edge(ref, names):
            q = names.index(i)
            return marked(ref[q : q + 1], ref[5:6])

        def corner():
            return marked(corner_ref[i - 7, 0:1], corner_ref[i - 7, 1:2])

        value = moved(value, lambda: x_edge(x_up_ref, X_UP), lambda: x_edge(x_down_ref, X_DOWN))
        if cy != 0:
            ref, names = (y_up_ref, Y_UP) if cy == 1 else (y_down_ref, Y_DOWN)
            edge = moved(marked(ref[names.index(i)], ref[5]), corner, corner)
            edge = pltpu.roll(edge, NZ, 1)
            value = pltpu.roll(value, NZ if cy == 1 else cols - NZ, 1)
            if cy == 1:
                value = jnp.concatenate(
                    [jnp.where(lower, edge, value[:, 0:128]), value[:, 128:]], axis=1
                )
            else:
                value = jnp.concatenate(
                    [value[:, : cols - 128], jnp.where(lower, value[:, cols - 128 :], edge)], axis=1
                )
        if cz != 0:
            value = pltpu.roll(value, 1 if cz == 1 else cols - 1, 1)
            blocked = (value == BLANK) | (height == (0 if cz == 1 else NZ - 1))
        else:
            blocked = value == BLANK
        value = jnp.where(blocked, post_ref[OPP[i]], value)
        out_ref[i] = jnp.where(is_solid, post_ref[i], value)


def call(kernel, out_shape, scratch=(), n_vmem=0, n_smem=0, smem_out=0, **params):
    spaces = [pltpu.SMEM] * n_smem + [pltpu.VMEM] * n_vmem
    outs = [pltpu.SMEM] * smem_out + [pltpu.VMEM] * (len(out_shape) - smem_out)
    return pl.pallas_call(
        kernel,
        out_shape=out_shape,
        in_specs=[pl.BlockSpec(memory_space=space) for space in spaces],
        out_specs=tuple(pl.BlockSpec(memory_space=space) for space in outs),
        scratch_shapes=list(scratch),
        compiler_params=pltpu.CompilerParams(vmem_limit_bytes=VMEM, **params),
    )


def on_device(
    populations,
    solid,
    link_cell,
    link_dir,
    link_owner,
    link_elem,
    elem_nodes,
    elem_grads,
    elem_area,
    elem_normal,
    node_mass,
    displacement,
    velocity,
):
    owners = lax.axis_size(("gx", "gy"))
    elements = elem_nodes.shape[1]
    rows, cols = solid.shape
    nodal = [x.reshape(-1, 128) for x in (displacement, velocity, node_mass)]

    def f32(*shape):
        return jax.ShapeDtypeStruct(shape, F32)

    halo_shapes = (f32(6, cols), f32(6, cols), f32(6, rows, 128), f32(6, rows, 128), f32(4, 2, 128))
    def i32(*shape):
        return jax.ShapeDtypeStruct(shape, jnp.int32)

    nx, ny = lax.axis_size("gx"), lax.axis_size("gy")
    owner = lax.optimization_barrier(link_owner.reshape(-1))
    key, code = lax.sort(
        (owner * elements + link_elem, link_dir * (rows * cols) + link_cell), num_keys=1, is_stable=False
    )
    key, code = key.reshape(-1, 128), code.reshape(-1, 128)
    count = key.shape[0]
    starts, elem, way = call(
        cut_kernel,
        (i32(8, 128), i32(ny, nx, 4, 128), i32(nx, ny, 4, 128)),
        scratch=[
            pltpu.VMEM((count + 8, 128), jnp.int32),
            pltpu.VMEM((count + 8, 128), jnp.int32),
            pltpu.VMEM((8, 128), jnp.int32),
            pltpu.SemaphoreType.DMA,
        ],
        n_vmem=2,
        smem_out=1,
    )(key, code)

    post, table, *rest = call(
        collide_kernel,
        (
            f32(*populations.shape),
            jax.ShapeDtypeStruct((256, 1152), BF16),
            *halo_shapes,
            f32(16, 128),
            f32(1, elements),
            i32(8, 128),
        ),
        n_vmem=5,
    )(populations, solid, nodal[0], elem_area.reshape(1, -1), starts)
    halo, (field, area, starts) = rest[:5], rest[5:]

    value, elem, way, *halo, counts, tension = call(
        exchange_kernel,
        (
            f32(owners, 4, 128),
            i32(nx, ny, 4, 128),
            i32(ny, nx, 4, 128),
            *halo_shapes,
            i32(8, 128),
            f32(32, 128),
        ),
        scratch=[
            pltpu.VMEM((RIM // 128, 128), F32),
            pltpu.VMEM((136, 128), F32),
            pltpu.VMEM((owners, 4, 128), F32),
            pltpu.VMEM((ny, nx, 4, 128), jnp.int32),
            pltpu.VMEM((nx, ny, 4, 128), jnp.int32),
            pltpu.SemaphoreType.REGULAR,
            pltpu.SemaphoreType.DMA((9,)),
            pltpu.SemaphoreType.DMA((9,)),
            pltpu.SemaphoreType.DMA((2,)),
            pltpu.SemaphoreType.DMA((2,)),
            pltpu.SemaphoreType.DMA((2,)),
            pltpu.SemaphoreType.DMA((2,)),
            pltpu.SemaphoreType.DMA,
            pltpu.SemaphoreType.DMA,
        ],
        n_smem=1,
        n_vmem=13,
        collective_id=0,
        has_side_effects=True,
    )(starts, code, table, elem, way, *halo, field, elem_nodes, elem_grads, area)

    element_force, load = call(
        force_kernel,
        (f32(3, elements), f32(1, elements)),
        scratch=[pltpu.VMEM((192, 128), F32), pltpu.SMEM((768,), jnp.int32)],
        n_smem=1,
        n_vmem=4,
    )(counts, value, elem.reshape(owners, 4, 128), way.reshape(owners, 4, 128), elem_normal)

    node, returned = call(
        facade_kernel,
        (f32(16, 128), f32(RIM // 128, 128)),
        scratch=[
            pltpu.VMEM((RIM // 128, 128), F32),
            pltpu.VMEM((RIM // 128, 128), F32),
            pltpu.SemaphoreType.DMA,
            pltpu.SemaphoreType.DMA,
        ],
        n_vmem=3,
        collective_id=1,
        has_side_effects=True,
    )(load, elem_nodes, tension)

    populations_out, displacement_out, velocity_out = call(
        pass_kernel,
        (f32(*populations.shape), f32(16, 128), f32(16, 128)),
        n_vmem=12,
    )(post, solid, *halo, node, returned, *nodal)
    return (populations_out, element_force, displacement_out.reshape(-1), velocity_out.reshape(-1))


def solution(mesh):
    in_specs = (
        P(None, "gx", "gy"),
        P("gx", "gy"),
        P(("gx", "gy")),
        P(("gx", "gy")),
        P(("gx", "gy"), None),
        P(("gx", "gy")),
        P(None, ("gx", "gy")),
        P(None, ("gx", "gy")),
        P(("gx", "gy")),
        P(None, ("gx", "gy")),
        P(("gx", "gy")),
        P(("gx", "gy")),
        P(("gx", "gy")),
    )
    out_specs = (P(None, "gx", "gy"), P(None, ("gx", "gy")), P(("gx", "gy")), P(("gx", "gy")))
    return jax.shard_map(
        on_device, mesh=mesh, in_specs=in_specs, out_specs=out_specs, check_vma=False
    )
```

```python
import functools

import jax
import jax.numpy as jnp
from jax import lax
from jax.experimental import pallas as pl
from jax.experimental.pallas import tpu as pltpu
from jax.sharding import PartitionSpec as P

NZ = 64
RIM = 512
BLANK = -1e30

SPEEDS = [
    (0, 0, 0),
    (1, 0, 0),
    (-1, 0, 0),
    (0, 1, 0),
    (0, -1, 0),
    (0, 0, 1),
    (0, 0, -1),
    (1, 1, 0),
    (-1, -1, 0),
    (1, -1, 0),
    (-1, 1, 0),
    (1, 0, 1),
    (-1, 0, -1),
    (1, 0, -1),
    (-1, 0, 1),
    (0, 1, 1),
    (0, -1, -1),
    (0, 1, -1),
    (0, -1, 1),
]
WEIGHTS = [1.0 / 3.0] + [1.0 / 18.0] * 6 + [1.0 / 36.0] * 12
OPP = [0, 2, 1, 4, 3, 6, 5, 8, 7, 10, 9, 12, 11, 14, 13, 16, 15, 18, 17]
X_UP = [i for i in range(19) if SPEEDS[i][0] == 1]
X_DOWN = [i for i in range(19) if SPEEDS[i][0] == -1]
Y_UP = [i for i in range(19) if SPEEDS[i][1] == 1]
Y_DOWN = [i for i in range(19) if SPEEDS[i][1] == -1]
relax_time = 0.8
time_step = 0.5
VMEM = 48 * 1024 * 1024
F32 = jnp.float32
BF16 = jnp.bfloat16
MESH = pl.DeviceIdType.MESH
FIRST = 4
SECOND = 12
GROUP = 8
LOT = 32


def halves(x):
    high = x.astype(BF16)
    return high, (x - high.astype(F32)).astype(BF16)


def signed_sum(terms):
    plus = [v for s, v in terms if s > 0]
    minus = [v for s, v in terms if s < 0]
    return functools.reduce(jnp.add, plus) - functools.reduce(jnp.add, minus)


def signed_sum_any(terms):
    total = None
    for s, v in terms:
        if total is None:
            total = v if s > 0 else -v
        else:
            total = total + v if s > 0 else total - v
    return total


def one_hot(index, size):
    rows = lax.broadcasted_iota(jnp.int16, (size, index.shape[1]), 0)
    return jnp.where(rows == index.astype(jnp.int16), jnp.ones((), BF16), jnp.zeros((), BF16))


def spread_rows(value_rows, index, size):
    rows = lax.broadcasted_iota(jnp.int16, (size, index.shape[1]), 0)
    mine = rows == index.astype(jnp.int16)
    return [jnp.where(mine, v, jnp.zeros((), BF16)) for v in value_rows]


def cut(starts_ref, o):
    lanes = lax.broadcasted_iota(jnp.int32, (8, 128), 1)
    subs = lax.broadcasted_iota(jnp.int32, (8, 128), 0)
    base = starts_ref[0, o]
    number = starts_ref[1, o] - base
    first = base >> 7
    offset = base & 127
    near = lanes < 128 - offset

    def window(ref):
        x = pltpu.roll(ref[pl.ds(first, 8), :], (128 - offset) & 127, 1)
        return jnp.where(near, x, pltpu.roll(x, 7, 0))

    return window, subs * 128 + lanes < number


def find_starts(owner):
    last = owner.T[127:128]
    lanes = lax.broadcasted_iota(jnp.int32, (1, 128), 1)
    previous = jnp.where(lanes == 0, -1.0, pltpu.roll(last, 1, 1))
    wanted = lax.broadcasted_iota(jnp.int32, (128, 128), 0).astype(F32)
    full = last < wanted
    split = jnp.where((last >= wanted) & (previous < wanted), 1.0, 0.0).astype(BF16)
    row = jnp.dot(split, (owner - 128.0).astype(BF16), preferred_element_type=F32)
    before = jnp.where(full, 128.0, 0.0) + jnp.where(row < wanted - 128.0, 1.0, 0.0)
    starts = lax.dot_general(
        jnp.ones((8, 128), BF16),
        before.astype(BF16),
        (((1,), (1,)), ((), ())),
        preferred_element_type=F32,
    ).astype(jnp.int32)
    lanes = lax.broadcasted_iota(jnp.int32, (8, 128), 1)
    subs = lax.broadcasted_iota(jnp.int32, (8, 128), 0)
    ends = jnp.where(lanes == 127, 128 * 128, pltpu.roll(starts, 127, 1))
    return jnp.where(subs == 0, starts, ends)


def cut_kernel(key_ref, code_ref, starts_ref, elem_ref, dir_ref, elem_s, dir_s, starts_v, sem):
    starts_v[...] = find_starts((key_ref[...] >> 12).astype(F32))
    copy = pltpu.make_async_copy(starts_v, starts_ref, sem)
    copy.start()
    count = key_ref.shape[0]
    elem_s[0:count, :] = key_ref[...] & 4095
    dir_s[0:count, :] = code_ref[...] >> 13
    elem_s[count : count + 8, :] = jnp.zeros((8, 128), jnp.int32)
    dir_s[count : count + 8, :] = jnp.zeros((8, 128), jnp.int32)
    copy.wait()
    ny, nx = elem_ref.shape[:2]

    def spread(o, carry):
        window, _ = cut(starts_ref, o)
        x, y = o // ny, lax.rem(o, ny)
        elem_ref[y, x] = window(elem_s)[0:4]
        dir_ref[x, y] = window(dir_s)[0:4]
        return carry

    lax.fori_loop(0, nx * ny, spread, 0, unroll=8)


def collide_kernel(
    popul_ref,
    solid_ref,
    displacement_ref,
    starts_ref,
    post_ref,
    table_ref,
    x_up_ref,
    x_down_ref,
    y_up_ref,
    y_down_ref,
    corner_ref,
    field_out,
    starts_out,
):
    rows, cols = solid_ref.shape
    field_out[...] = displacement_ref[...]
    starts_out[...] = starts_ref[...]
    for t in range(cols // 128):
        at = pl.ds(128 * t, 128)
        f = [popul_ref[i, :, at] for i in range(19)]
        is_solid = solid_ref[:, at] != 0
        density = functools.reduce(jnp.add, f)
        inverse = 1.0 / density
        flow = [
            signed_sum([(SPEEDS[i][k], f[i]) for i in range(19) if SPEEDS[i][k] != 0]) * inverse
            for k in range(3)
        ]
        square = flow[0] * flow[0] + flow[1] * flow[1] + flow[2] * flow[2]
        rest = 1.0 - 1.5 * square
        keep = 1.0 - 1.0 / relax_time
        for i in range(19):
            if i != 0 and OPP[i] < i:
                continue
            scaled = (WEIGHTS[i] / relax_time) * density
            if i == 0:
                new = keep * f[0] + scaled * rest
                post_ref[0, :, at] = jnp.where(is_solid, f[0], new)
                continue
            along = signed_sum_any([(SPEEDS[i][k], flow[k]) for k in range(3) if SPEEDS[i][k] != 0])
            even = scaled * (rest + 4.5 * along * along)
            odd = scaled * (3.0 * along)
            j = OPP[i]
            post_ref[i, :, at] = jnp.where(is_solid, f[i], keep * f[i] + (even + odd))
            post_ref[j, :, at] = jnp.where(is_solid, f[j], keep * f[j] + (even - odd))
    for pair in range(9):
        block = jnp.concatenate(
            [
                post_ref[d, :, 128 * t : 128 * t + 128]
                for d in (1 + 2 * pair, 2 + 2 * pair)
                for t in range(cols // 128)
            ],
            axis=0,
        )
        turned = block.T
        rolled = pltpu.roll(turned, 64, 1)
        lower = lax.broadcasted_iota(jnp.int32, (16, 128), 1) < 64
        for second in range(2):
            near, far = (rolled, turned) if second else (turned, rolled)
            row = 16 * (2 * pair + second)
            for p in range(4):
                piece = jnp.where(lower, near[32 * p : 32 * p + 16], far[32 * p + 16 : 32 * p + 32])
                high, low = halves(2.0 * piece)
                table_ref[row : row + 16, 128 * p : 128 * p + 128] = high
                table_ref[288 + row : 304 + row, 128 * p : 128 * p + 128] = low

    flag = solid_ref[...].astype(F32)
    for q in range(5):
        x_up_ref[q : q + 1] = post_ref[X_UP[q], rows - 1 : rows]
        x_down_ref[q : q + 1] = post_ref[X_DOWN[q], 0:1]
        y_up_ref[q] = post_ref[Y_UP[q], :, cols - 128 : cols]
        y_down_ref[q] = post_ref[Y_DOWN[q], :, 0:128]
    x_up_ref[5:6] = flag[rows - 1 : rows]
    x_down_ref[5:6] = flag[0:1]
    y_up_ref[5] = flag[:, cols - 128 : cols]
    y_down_ref[5] = flag[:, 0:128]
    for q in range(4):
        cx, cy, _ = SPEEDS[7 + q]
        row = slice(rows - 1, rows) if cx == 1 else slice(0, 1)
        lane = slice(cols - 128, cols) if cy == 1 else slice(0, 128)
        corner_ref[q, 0:1] = post_ref[7 + q, row, lane]
        corner_ref[q, 1:2] = flag[row, lane]


def exchange_kernel(
    starts_ref,
    code_ref,
    table_ref,
    elem_ref,
    dir_ref,
    x_up_ref,
    x_down_ref,
    y_up_ref,
    y_down_ref,
    corner_ref,
    displacement_ref,
    nodes_ref,
    grads_ref,
    area_ref,
    normal_ref,
    velocity_ref,
    mass_ref,
    x_up_out,
    x_down_out,
    y_up_out,
    y_down_out,
    corner_out,
    force_out,
    displacement_out,
    velocity_out,
    rim_s,
    val_s,
    value_s,
    value_in,
    elem_relay,
    dir_relay,
    elem_in,
    dir_in,
    tension_s,
    load_s,
    acc,
    back_s,
    return_s,
    all_in,
    near_send,
    near_recv,
    elem_send,
    elem_recv,
    dir_send,
    dir_recv,
    value_send,
    value_recv,
    back_send,
    back_recv,
):
    count = code_ref.shape[0]
    gx, gy = lax.axis_index("gx"), lax.axis_index("gy")
    nx, ny = lax.axis_size("gx"), lax.axis_size("gy")
    owners = nx * ny
    me = gx * ny + gy

    def place(other):
        return (other // ny, lax.rem(other, ny))

    barrier = pltpu.get_barrier_semaphore()

    row_peers = [(gx, lax.rem(gy + d, ny)) for d in range(1, ny)]
    column_peers = [(lax.rem(gx + d, nx), gy) for d in range(1, nx)]
    for other in row_peers + column_peers:
        pl.semaphore_signal(barrier, inc=1, device_id=other, device_id_type=MESH)

    span = 8

    def gather(b, carry):
        code = code_ref[pl.ds(pl.multiple_of(span * b, span), span), :]
        code = jnp.concatenate([code[r : r + 1] for r in range(span)], axis=1)
        cell = code & 8191
        column = ((cell >> 4) & 7) * 64 + ((cell >> 7) & 7) * 8 + (cell >> 10)
        row = ((code >> 13) - 1) * 16 + (cell & 15)
        hot = one_hot(column, table_ref.shape[1])
        found = jnp.dot(table_ref[...], hot, preferred_element_type=F32)
        both = found[0:288] + found[288:576]
        rows = lax.broadcasted_iota(jnp.int32, both.shape, 0)
        got = jnp.sum(jnp.where(rows == row, both, 0.0), axis=0, keepdims=True)
        for r in range(span):
            val_s[pl.ds(span * b + r, 1), :] = got[:, 128 * r : 128 * r + 128]
        return carry

    blocks = count // span
    val_s[count : count + 8, :] = jnp.zeros((8, 128), F32)

    lax.fori_loop(0, FIRST, gather, 0, unroll=2)
    pl.semaphore_wait(barrier, nx + ny - 2)
    for other in column_peers:
        pl.semaphore_signal(all_in, inc=1, device_id=other, device_id_type=MESH)

    right, left = lax.rem(gx + 1, nx), lax.rem(gx + nx - 1, nx)
    above, below = lax.rem(gy + 1, ny), lax.rem(gy + ny - 1, ny)
    moves = [
        (x_up_ref, x_up_out, (right, gy)),
        (x_down_ref, x_down_out, (left, gy)),
        (y_up_ref, y_up_out, (gx, above)),
        (y_down_ref, y_down_out, (gx, below)),
        (corner_ref.at[0], corner_out.at[0], (right, above)),
        (corner_ref.at[1], corner_out.at[1], (left, below)),
        (corner_ref.at[2], corner_out.at[2], (right, below)),
        (corner_ref.at[3], corner_out.at[3], (left, above)),
        (displacement_ref.at[0 : RIM // 128], rim_s, place(lax.rem(me + owners - 1, owners))),
    ]
    def remote(src, dst, send_sem, recv_sem, other):
        return pltpu.make_async_remote_copy(
            src_ref=src,
            dst_ref=dst,
            send_sem=send_sem,
            recv_sem=recv_sem,
            device_id=other,
            device_id_type=MESH,
        )

    def settle(buffer, number, send_sem, recv_sem):
        part = buffer.at[pl.ds(0, number)]
        remote(part, part, send_sem, recv_sem, (right, gy)).wait()

    for other in row_peers:
        remote(elem_ref.at[other[1]], elem_relay.at[gy], elem_send.at[0], elem_recv.at[0], other).start()
    for other in column_peers:
        remote(dir_ref.at[other[0]], dir_relay.at[gx], dir_send.at[0], dir_recv.at[0], other).start()
    elem_relay[gy] = elem_ref[gy]
    dir_relay[gx] = dir_ref[gx]
    lax.fori_loop(FIRST, SECOND, gather, 0, unroll=2)
    settle(elem_relay, ny - 1, elem_send.at[0], elem_recv.at[0])
    settle(dir_relay, nx - 1, dir_send.at[0], dir_recv.at[0])
    for other in column_peers:
        remote(
            elem_relay.at[:, other[0]], elem_in.at[gx], elem_send.at[1], elem_recv.at[1], other
        ).start()
    for other in row_peers:
        remote(
            dir_relay.at[:, other[1]], dir_in.at[gy], dir_send.at[1], dir_recv.at[1], other
        ).start()
    elem_in[gx] = elem_relay[:, gx]
    dir_in[gy] = dir_relay[:, gy]
    pl.semaphore_wait(all_in, nx - 1)
    near = [
        remote(src, dst, near_send.at[q], near_recv.at[q], to)
        for q, (src, dst, to) in enumerate(moves)
    ]
    for copy in near:
        copy.start()
    lax.fori_loop(SECOND, blocks, gather, 0, unroll=2)

    def fill(o):
        window, valid = cut(starts_ref, o)
        return jnp.where(valid, window(val_s), 0.0)[0:4]

    value_in[me] = fill(me)

    def send_values(first, number, lot):
        others = [lax.rem(me + first + r, owners) for r in range(number)]
        for other in others:
            value_s[other] = fill(other)
        for other in others:
            remote(
                value_s.at[other], value_in.at[me], value_send, value_recv.at[lot], place(other)
            ).start()

    def send_group(g, carry):
        send_values(1 + GROUP * g, GROUP, g // (LOT // GROUP))
        return carry

    groups = (owners - 1) // GROUP
    lots = owners // LOT
    lax.fori_loop(0, groups, send_group, 0)
    send_values(1 + GROUP * groups, owners - 1 - GROUP * groups, lots - 1)

    for copy in near:
        copy.wait()

    tension_s[...] = node_tension(displacement_ref, rim_s, nodes_ref, grads_ref, area_ref)
    settle(elem_in, nx - 1, elem_send.at[1], elem_recv.at[1])
    settle(dir_in, ny - 1, dir_send.at[1], dir_recv.at[1])
    acc[...] = jnp.zeros_like(acc)

    def arrived(number, lot):
        part = value_in.at[pl.ds(0, number)]
        remote(part, part, value_send, value_recv.at[lot], (right, gy)).wait_recv()

    def add_lot(lot):
        values, elems, ways = [], [], []
        for r in range(LOT):
            source = lax.rem(me + 2 * owners - (LOT * lot + r + 1), owners)
            x, y = place(source)
            values.append(value_in[source])
            elems.append(elem_in[x, y])
            ways.append(dir_in[y, x])
        v, elem, way = [
            jnp.concatenate([x[r : r + 1] for x in group for r in range(4)], axis=1)
            for group in (values, elems, ways)
        ]
        bit = jnp.left_shift(jnp.ones_like(way), way)
        parts = []
        for k in range(3):
            plus = sum(1 << i for i in range(19) if SPEEDS[i][k] == 1)
            minus = sum(1 << i for i in range(19) if SPEEDS[i][k] == -1)
            part = jnp.where((bit & plus) != 0, v, jnp.where((bit & minus) != 0, -v, 0.0))
            parts.extend(halves(part))
        left = jnp.concatenate(spread_rows(parts, elem >> 7, 32), axis=0)
        acc[...] += lax.dot_general(
            left, one_hot(elem & 127, 128), (((1,), (1,)), ((), ())), preferred_element_type=F32
        )

    def take_lot(lot, carry):
        arrived(LOT, lot)
        add_lot(lot)
        return carry

    lax.fori_loop(0, lots - 1, take_lot, 0)
    arrived(LOT - 1, lots - 1)
    add_lot(lots - 1)

    forces = [acc[64 * k : 64 * k + 32] + acc[64 * k + 32 : 64 * k + 64] for k in range(3)]
    for h in range(32):
        at = slice(128 * h, 128 * h + 128)
        lines = [f[h : h + 1] for f in forces]
        force_out[:, at] = jnp.concatenate(lines, axis=0)
        load_s[:, at] = sum(normal_ref[k : k + 1, at] * lines[k] for k in range(3)) / 3.0
    node = node_sums(nodes_ref, [load_s[...]] * 3) - tension_s[...]
    back_s[...] = node[16:20]
    back = remote(back_s, return_s, back_send, back_recv, place(lax.rem(me + 1, owners)))
    back.start()
    sent = value_s.at[pl.ds(0, owners - 1)]
    remote(sent, sent, value_send, value_recv.at[0], (right, gy)).wait_send()
    back.wait()
    returned = jnp.concatenate([return_s[...], jnp.zeros((12, 128), F32)], axis=0)
    speed = velocity_ref[...] + time_step * (node[0:16] + returned) / mass_ref[...]
    velocity_out[...] = speed
    displacement_out[...] = displacement_ref[...] + time_step * speed


SPAN = 1024


def node_sums(nodes_ref, rows):
    total = jnp.zeros((64, 128), F32)
    for j in range(3):
        for b in range(nodes_ref.shape[1] // SPAN):
            at = slice(SPAN * b, SPAN * b + SPAN)
            n = nodes_ref[j : j + 1, at]
            left = jnp.concatenate(spread_rows(halves(rows[j][:, at]), n >> 7, 32), axis=0)
            total = total + lax.dot_general(
                left, one_hot(n & 127, 128), (((1,), (1,)), ((), ())), preferred_element_type=F32
            )
    return total[0:32] + total[32:64]


def node_tension(displacement_ref, rim_ref, nodes_ref, grads_ref, area_ref):
    field = jnp.concatenate([displacement_ref[...], rim_ref[...], jnp.zeros((12, 128), F32)], axis=0)
    table = jnp.concatenate(halves(field), axis=0)
    values = []
    for j in range(3):
        pieces = []
        for b in range(nodes_ref.shape[1] // SPAN):
            n = nodes_ref[j : j + 1, SPAN * b : SPAN * b + SPAN]
            found = jnp.dot(table, one_hot(n & 127, 128), preferred_element_type=F32)
            both = found[0:24] + found[32:56]
            rows = lax.broadcasted_iota(jnp.int32, both.shape, 0)
            pieces.append(jnp.sum(jnp.where(rows == (n >> 7), both, 0.0), axis=0, keepdims=True))
        values.append(jnp.concatenate(pieces, axis=1))
    g = [grads_ref[k : k + 1] for k in range(6)]
    area = area_ref[...]
    slope_x = area * (g[0] * values[0] + g[2] * values[1] + g[4] * values[2])
    slope_y = area * (g[1] * values[0] + g[3] * values[1] + g[5] * values[2])
    return node_sums(nodes_ref, [g[2 * j] * slope_x + g[2 * j + 1] * slope_y for j in range(3)])


def pass_kernel(
    post_ref,
    solid_ref,
    x_up_ref,
    x_down_ref,
    y_up_ref,
    y_down_ref,
    corner_ref,
    displacement_ref,
    velocity_ref,
    force_ref,
    out_ref,
    displacement_out,
    velocity_out,
    force_out,
):
    force_out[...] = force_ref[...]
    velocity_out[...] = velocity_ref[...]
    displacement_out[...] = displacement_ref[...]
    is_solid = solid_ref[...] != 0
    rows, cols = is_solid.shape
    height = lax.broadcasted_iota(jnp.int32, (rows, cols), 1) % NZ
    lower = lax.broadcasted_iota(jnp.int32, (rows, 128), 1) < NZ

    def marked(value, solid):
        return jnp.where(solid != 0.0, BLANK, value)

    for i in range(19):
        cx, cy, cz = SPEEDS[i]
        if i == 0:
            out_ref[0] = post_ref[0]
            continue
        value = jnp.where(is_solid, BLANK, post_ref[i])

        def moved(core, first, last):
            if cx == 1:
                return jnp.concatenate([first(), core[0 : rows - 1]], axis=0)
            if cx == -1:
                return jnp.concatenate([core[1:rows], last()], axis=0)
            return core

        def x_edge(ref, names):
            q = names.index(i)
            return marked(ref[q : q + 1], ref[5:6])

        def corner():
            return marked(corner_ref[i - 7, 0:1], corner_ref[i - 7, 1:2])

        value = moved(value, lambda: x_edge(x_up_ref, X_UP), lambda: x_edge(x_down_ref, X_DOWN))
        if cy != 0:
            ref, names = (y_up_ref, Y_UP) if cy == 1 else (y_down_ref, Y_DOWN)
            edge = moved(marked(ref[names.index(i)], ref[5]), corner, corner)
            edge = pltpu.roll(edge, NZ, 1)
            value = pltpu.roll(value, NZ if cy == 1 else cols - NZ, 1)
            if cy == 1:
                value = jnp.concatenate(
                    [jnp.where(lower, edge, value[:, 0:128]), value[:, 128:]], axis=1
                )
            else:
                value = jnp.concatenate(
                    [value[:, : cols - 128], jnp.where(lower, value[:, cols - 128 :], edge)], axis=1
                )
        if cz != 0:
            value = pltpu.roll(value, 1 if cz == 1 else cols - 1, 1)
            blocked = (value == BLANK) | (height == (0 if cz == 1 else NZ - 1))
        else:
            blocked = value == BLANK
        value = jnp.where(blocked, post_ref[OPP[i]], value)
        out_ref[i] = jnp.where(is_solid, post_ref[i], value)


def call(kernel, out_shape, scratch=(), n_vmem=0, n_smem=0, smem_out=0, **params):
    spaces = [pltpu.SMEM] * n_smem + [pltpu.VMEM] * n_vmem
    outs = [pltpu.SMEM] * smem_out + [pltpu.VMEM] * (len(out_shape) - smem_out)
    return pl.pallas_call(
        kernel,
        out_shape=out_shape,
        in_specs=[pl.BlockSpec(memory_space=space) for space in spaces],
        out_specs=tuple(pl.BlockSpec(memory_space=space) for space in outs),
        scratch_shapes=list(scratch),
        compiler_params=pltpu.CompilerParams(vmem_limit_bytes=VMEM, **params),
    )


def on_device(
    populations,
    solid,
    link_cell,
    link_dir,
    link_owner,
    link_elem,
    elem_nodes,
    elem_grads,
    elem_area,
    elem_normal,
    node_mass,
    displacement,
    velocity,
):
    owners = lax.axis_size(("gx", "gy"))
    elements = elem_nodes.shape[1]
    rows, cols = solid.shape
    nodal = [x.reshape(-1, 128) for x in (displacement, velocity, node_mass)]

    def f32(*shape):
        return jax.ShapeDtypeStruct(shape, F32)

    halo_shapes = (f32(6, cols), f32(6, cols), f32(6, rows, 128), f32(6, rows, 128), f32(4, 2, 128))
    def i32(*shape):
        return jax.ShapeDtypeStruct(shape, jnp.int32)

    nx, ny = lax.axis_size("gx"), lax.axis_size("gy")
    owner = lax.optimization_barrier(link_owner.reshape(-1))
    key, code = lax.sort(
        (owner * elements + link_elem, link_dir * (rows * cols) + link_cell), num_keys=1, is_stable=False
    )
    key, code = key.reshape(-1, 128), code.reshape(-1, 128)
    count = key.shape[0]
    starts, elem, way = call(
        cut_kernel,
        (i32(8, 128), i32(ny, nx, 4, 128), i32(nx, ny, 4, 128)),
        scratch=[
            pltpu.VMEM((count + 8, 128), jnp.int32),
            pltpu.VMEM((count + 8, 128), jnp.int32),
            pltpu.VMEM((8, 128), jnp.int32),
            pltpu.SemaphoreType.DMA,
        ],
        n_vmem=2,
        smem_out=1,
    )(key, code)

    post, table, *rest = call(
        collide_kernel,
        (
            f32(*populations.shape),
            jax.ShapeDtypeStruct((576, 512), BF16),
            *halo_shapes,
            f32(16, 128),
            i32(8, 128),
        ),
        n_vmem=4,
    )(populations, solid, nodal[0], starts)
    halo, (field, starts) = rest[:5], rest[5:]

    *halo, force, moved, speed = call(
        exchange_kernel,
        (*halo_shapes, f32(3, elements), f32(16, 128), f32(16, 128)),
        scratch=[
            pltpu.VMEM((RIM // 128, 128), F32),
            pltpu.VMEM((136, 128), F32),
            pltpu.VMEM((owners, 4, 128), F32),
            pltpu.VMEM((owners, 4, 128), F32),
            pltpu.VMEM((ny, nx, 4, 128), jnp.int32),
            pltpu.VMEM((nx, ny, 4, 128), jnp.int32),
            pltpu.VMEM((nx, ny, 4, 128), jnp.int32),
            pltpu.VMEM((ny, nx, 4, 128), jnp.int32),
            pltpu.VMEM((32, 128), F32),
            pltpu.VMEM((1, elements), F32),
            pltpu.VMEM((192, 128), F32),
            pltpu.VMEM((RIM // 128, 128), F32),
            pltpu.VMEM((RIM // 128, 128), F32),
            pltpu.SemaphoreType.REGULAR,
            pltpu.SemaphoreType.DMA((9,)),
            pltpu.SemaphoreType.DMA((9,)),
            pltpu.SemaphoreType.DMA((2,)),
            pltpu.SemaphoreType.DMA((2,)),
            pltpu.SemaphoreType.DMA((2,)),
            pltpu.SemaphoreType.DMA((2,)),
            pltpu.SemaphoreType.DMA,
            pltpu.SemaphoreType.DMA((owners // LOT,)),
            pltpu.SemaphoreType.DMA,
            pltpu.SemaphoreType.DMA,
        ],
        n_smem=1,
        n_vmem=16,
        collective_id=0,
        has_side_effects=True,
    )(
        starts,
        code,
        table,
        elem,
        way,
        *halo,
        field,
        elem_nodes,
        elem_grads,
        elem_area.reshape(1, -1),
        elem_normal,
        *nodal[1:],
    )

    populations_out, displacement_out, velocity_out, element_force = call(
        pass_kernel,
        (f32(*populations.shape), f32(16, 128), f32(16, 128), f32(3, elements)),
        n_vmem=10,
    )(post, solid, *halo, moved, speed, force)
    return (populations_out, element_force, displacement_out.reshape(-1), velocity_out.reshape(-1))


def solution(mesh):
    in_specs = (
        P(None, "gx", "gy"),
        P("gx", "gy"),
        P(("gx", "gy")),
        P(("gx", "gy")),
        P(("gx", "gy"), None),
        P(("gx", "gy")),
        P(None, ("gx", "gy")),
        P(None, ("gx", "gy")),
        P(("gx", "gy")),
        P(None, ("gx", "gy")),
        P(("gx", "gy")),
        P(("gx", "gy")),
        P(("gx", "gy")),
    )
    out_specs = (P(None, "gx", "gy"), P(None, ("gx", "gy")), P(("gx", "gy")), P(("gx", "gy")))
    return jax.shard_map(
        on_device, mesh=mesh, in_specs=in_specs, out_specs=out_specs, check_vma=False
    )
```

```python
import functools

import jax
import jax.numpy as jnp
from jax import lax
from jax.experimental import pallas as pl
from jax.experimental.pallas import tpu as pltpu
from jax.sharding import PartitionSpec as P

NZ = 64
RIM = 512
BLANK = -1e30

SPEEDS = [
    (0, 0, 0),
    (1, 0, 0),
    (-1, 0, 0),
    (0, 1, 0),
    (0, -1, 0),
    (0, 0, 1),
    (0, 0, -1),
    (1, 1, 0),
    (-1, -1, 0),
    (1, -1, 0),
    (-1, 1, 0),
    (1, 0, 1),
    (-1, 0, -1),
    (1, 0, -1),
    (-1, 0, 1),
    (0, 1, 1),
    (0, -1, -1),
    (0, 1, -1),
    (0, -1, 1),
]
WEIGHTS = [1.0 / 3.0] + [1.0 / 18.0] * 6 + [1.0 / 36.0] * 12
OPP = [0, 2, 1, 4, 3, 6, 5, 8, 7, 10, 9, 12, 11, 14, 13, 16, 15, 18, 17]
X_UP = [i for i in range(19) if SPEEDS[i][0] == 1]
X_DOWN = [i for i in range(19) if SPEEDS[i][0] == -1]
Y_UP = [i for i in range(19) if SPEEDS[i][1] == 1]
Y_DOWN = [i for i in range(19) if SPEEDS[i][1] == -1]
relax_time = 0.8
time_step = 0.5
VMEM = 48 * 1024 * 1024
F32 = jnp.float32
BF16 = jnp.bfloat16
MESH = pl.DeviceIdType.MESH
FIRST = 4
SECOND = 12
GROUP = 8
LOT = 32


def halves(x):
    high = x.astype(BF16)
    return high, (x - high.astype(F32)).astype(BF16)


def signed_sum(terms):
    plus = [v for s, v in terms if s > 0]
    minus = [v for s, v in terms if s < 0]
    return functools.reduce(jnp.add, plus) - functools.reduce(jnp.add, minus)


def signed_sum_any(terms):
    total = None
    for s, v in terms:
        if total is None:
            total = v if s > 0 else -v
        else:
            total = total + v if s > 0 else total - v
    return total


def one_hot(index, size):
    rows = lax.broadcasted_iota(jnp.int16, (size, index.shape[1]), 0)
    return jnp.where(rows == index.astype(jnp.int16), jnp.ones((), BF16), jnp.zeros((), BF16))


def spread_rows(value_rows, index, size):
    rows = lax.broadcasted_iota(jnp.int16, (size, index.shape[1]), 0)
    mine = rows == index.astype(jnp.int16)
    return [jnp.where(mine, v, jnp.zeros((), BF16)) for v in value_rows]


def cut(starts_ref, o):
    lanes = lax.broadcasted_iota(jnp.int32, (8, 128), 1)
    subs = lax.broadcasted_iota(jnp.int32, (8, 128), 0)
    base = starts_ref[0, o]
    number = starts_ref[1, o] - base
    first = base >> 7
    offset = base & 127
    near = lanes < 128 - offset

    def window(ref):
        x = pltpu.roll(ref[pl.ds(first, 8), :], (128 - offset) & 127, 1)
        return jnp.where(near, x, pltpu.roll(x, 7, 0))

    return window, subs * 128 + lanes < number


def find_starts(owner):
    last = owner.T[127:128]
    lanes = lax.broadcasted_iota(jnp.int32, (1, 128), 1)
    previous = jnp.where(lanes == 0, -1.0, pltpu.roll(last, 1, 1))
    wanted = lax.broadcasted_iota(jnp.int32, (128, 128), 0).astype(F32)
    full = last < wanted
    split = jnp.where((last >= wanted) & (previous < wanted), 1.0, 0.0).astype(BF16)
    row = jnp.dot(split, (owner - 128.0).astype(BF16), preferred_element_type=F32)
    before = jnp.where(full, 128.0, 0.0) + jnp.where(row < wanted - 128.0, 1.0, 0.0)
    starts = lax.dot_general(
        jnp.ones((8, 128), BF16),
        before.astype(BF16),
        (((1,), (1,)), ((), ())),
        preferred_element_type=F32,
    ).astype(jnp.int32)
    lanes = lax.broadcasted_iota(jnp.int32, (8, 128), 1)
    subs = lax.broadcasted_iota(jnp.int32, (8, 128), 0)
    ends = jnp.where(lanes == 127, 128 * 128, pltpu.roll(starts, 127, 1))
    return jnp.where(subs == 0, starts, ends)


def cut_kernel(key_ref, code_ref, starts_ref, elem_ref, dir_ref, elem_s, dir_s, starts_v, sem):
    starts_v[...] = find_starts((key_ref[...] >> 12).astype(F32))
    copy = pltpu.make_async_copy(starts_v, starts_ref, sem)
    copy.start()
    count = key_ref.shape[0]
    elem_s[0:count, :] = key_ref[...] & 4095
    dir_s[0:count, :] = code_ref[...] >> 13
    elem_s[count : count + 8, :] = jnp.zeros((8, 128), jnp.int32)
    dir_s[count : count + 8, :] = jnp.zeros((8, 128), jnp.int32)
    copy.wait()
    ny, nx = elem_ref.shape[:2]

    def spread(o, carry):
        window, _ = cut(starts_ref, o)
        x, y = o // ny, lax.rem(o, ny)
        elem_ref[y, x] = window(elem_s)[0:4]
        dir_ref[x, y] = window(dir_s)[0:4]
        return carry

    lax.fori_loop(0, nx * ny, spread, 0, unroll=8)


def collide_kernel(
    popul_ref,
    solid_ref,
    displacement_ref,
    starts_ref,
    post_ref,
    table_ref,
    x_up_ref,
    x_down_ref,
    y_up_ref,
    y_down_ref,
    corner_ref,
    field_out,
    starts_out,
):
    rows, cols = solid_ref.shape
    field_out[...] = displacement_ref[...]
    starts_out[...] = starts_ref[...]
    for t in range(cols // 128):
        at = pl.ds(128 * t, 128)
        f = [popul_ref[i, :, at] for i in range(19)]
        is_solid = solid_ref[:, at] != 0
        density = functools.reduce(jnp.add, f)
        inverse = 1.0 / density
        flow = [
            signed_sum([(SPEEDS[i][k], f[i]) for i in range(19) if SPEEDS[i][k] != 0]) * inverse
            for k in range(3)
        ]
        square = flow[0] * flow[0] + flow[1] * flow[1] + flow[2] * flow[2]
        rest = 1.0 - 1.5 * square
        keep = 1.0 - 1.0 / relax_time
        for i in range(19):
            if i != 0 and OPP[i] < i:
                continue
            scaled = (WEIGHTS[i] / relax_time) * density
            if i == 0:
                new = keep * f[0] + scaled * rest
                post_ref[0, :, at] = jnp.where(is_solid, f[0], new)
                continue
            along = signed_sum_any([(SPEEDS[i][k], flow[k]) for k in range(3) if SPEEDS[i][k] != 0])
            even = scaled * (rest + 4.5 * along * along)
            odd = scaled * (3.0 * along)
            j = OPP[i]
            post_ref[i, :, at] = jnp.where(is_solid, f[i], keep * f[i] + (even + odd))
            post_ref[j, :, at] = jnp.where(is_solid, f[j], keep * f[j] + (even - odd))
    for pair in range(9):
        block = jnp.concatenate(
            [
                post_ref[d, :, 128 * t : 128 * t + 128]
                for d in (1 + 2 * pair, 2 + 2 * pair)
                for t in range(cols // 128)
            ],
            axis=0,
        )
        turned = block.T
        rolled = pltpu.roll(turned, 64, 1)
        lower = lax.broadcasted_iota(jnp.int32, (16, 128), 1) < 64
        for second in range(2):
            near, far = (rolled, turned) if second else (turned, rolled)
            row = 16 * (2 * pair + second)
            for p in range(4):
                piece = jnp.where(lower, near[32 * p : 32 * p + 16], far[32 * p + 16 : 32 * p + 32])
                high, low = halves(2.0 * piece)
                table_ref[row : row + 16, 128 * p : 128 * p + 128] = high
                table_ref[288 + row : 304 + row, 128 * p : 128 * p + 128] = low

    flag = solid_ref[...].astype(F32)
    for q in range(5):
        x_up_ref[q : q + 1] = post_ref[X_UP[q], rows - 1 : rows]
        x_down_ref[q : q + 1] = post_ref[X_DOWN[q], 0:1]
        y_up_ref[q] = post_ref[Y_UP[q], :, cols - 128 : cols]
        y_down_ref[q] = post_ref[Y_DOWN[q], :, 0:128]
    x_up_ref[5:6] = flag[rows - 1 : rows]
    x_down_ref[5:6] = flag[0:1]
    y_up_ref[5] = flag[:, cols - 128 : cols]
    y_down_ref[5] = flag[:, 0:128]
    for q in range(4):
        cx, cy, _ = SPEEDS[7 + q]
        row = slice(rows - 1, rows) if cx == 1 else slice(0, 1)
        lane = slice(cols - 128, cols) if cy == 1 else slice(0, 128)
        corner_ref[q, 0:1] = post_ref[7 + q, row, lane]
        corner_ref[q, 1:2] = flag[row, lane]


def exchange_kernel(
    starts_ref,
    code_ref,
    table_ref,
    elem_ref,
    dir_ref,
    x_up_ref,
    x_down_ref,
    y_up_ref,
    y_down_ref,
    corner_ref,
    displacement_ref,
    nodes_ref,
    grads_ref,
    area_ref,
    normal_ref,
    velocity_ref,
    mass_ref,
    post_ref,
    solid_ref,
    popul_out,
    force_out,
    displacement_out,
    velocity_out,
    x_up_out,
    x_down_out,
    y_up_out,
    y_down_out,
    corner_out,
    rim_s,
    val_s,
    value_s,
    value_in,
    elem_relay,
    dir_relay,
    elem_in,
    dir_in,
    tension_s,
    load_s,
    acc,
    back_s,
    return_s,
    all_in,
    near_send,
    near_recv,
    elem_send,
    elem_recv,
    dir_send,
    dir_recv,
    value_send,
    value_recv,
    back_send,
    back_recv,
):
    count = code_ref.shape[0]
    gx, gy = lax.axis_index("gx"), lax.axis_index("gy")
    nx, ny = lax.axis_size("gx"), lax.axis_size("gy")
    owners = nx * ny
    me = gx * ny + gy

    def place(other):
        return (other // ny, lax.rem(other, ny))

    barrier = pltpu.get_barrier_semaphore()

    row_peers = [(gx, lax.rem(gy + d, ny)) for d in range(1, ny)]
    column_peers = [(lax.rem(gx + d, nx), gy) for d in range(1, nx)]
    for other in row_peers + column_peers:
        pl.semaphore_signal(barrier, inc=1, device_id=other, device_id_type=MESH)

    span = 8

    def gather(b, carry):
        code = code_ref[pl.ds(pl.multiple_of(span * b, span), span), :]
        code = jnp.concatenate([code[r : r + 1] for r in range(span)], axis=1)
        cell = code & 8191
        column = ((cell >> 4) & 7) * 64 + ((cell >> 7) & 7) * 8 + (cell >> 10)
        row = ((code >> 13) - 1) * 16 + (cell & 15)
        hot = one_hot(column, table_ref.shape[1])
        found = jnp.dot(table_ref[...], hot, preferred_element_type=F32)
        both = found[0:288] + found[288:576]
        rows = lax.broadcasted_iota(jnp.int32, both.shape, 0)
        got = jnp.sum(jnp.where(rows == row, both, 0.0), axis=0, keepdims=True)
        for r in range(span):
            val_s[pl.ds(span * b + r, 1), :] = got[:, 128 * r : 128 * r + 128]
        return carry

    blocks = count // span
    val_s[count : count + 8, :] = jnp.zeros((8, 128), F32)

    lax.fori_loop(0, FIRST, gather, 0, unroll=2)
    pl.semaphore_wait(barrier, nx + ny - 2)
    for other in column_peers:
        pl.semaphore_signal(all_in, inc=1, device_id=other, device_id_type=MESH)

    right, left = lax.rem(gx + 1, nx), lax.rem(gx + nx - 1, nx)
    above, below = lax.rem(gy + 1, ny), lax.rem(gy + ny - 1, ny)
    moves = [
        (x_up_ref, x_up_out, (right, gy)),
        (x_down_ref, x_down_out, (left, gy)),
        (y_up_ref, y_up_out, (gx, above)),
        (y_down_ref, y_down_out, (gx, below)),
        (corner_ref.at[0], corner_out.at[0], (right, above)),
        (corner_ref.at[1], corner_out.at[1], (left, below)),
        (corner_ref.at[2], corner_out.at[2], (right, below)),
        (corner_ref.at[3], corner_out.at[3], (left, above)),
        (displacement_ref.at[0 : RIM // 128], rim_s, place(lax.rem(me + owners - 1, owners))),
    ]
    def remote(src, dst, send_sem, recv_sem, other):
        return pltpu.make_async_remote_copy(
            src_ref=src,
            dst_ref=dst,
            send_sem=send_sem,
            recv_sem=recv_sem,
            device_id=other,
            device_id_type=MESH,
        )

    def settle(buffer, number, send_sem, recv_sem):
        part = buffer.at[pl.ds(0, number)]
        remote(part, part, send_sem, recv_sem, (right, gy)).wait()

    for other in row_peers:
        remote(elem_ref.at[other[1]], elem_relay.at[gy], elem_send.at[0], elem_recv.at[0], other).start()
    for other in column_peers:
        remote(dir_ref.at[other[0]], dir_relay.at[gx], dir_send.at[0], dir_recv.at[0], other).start()
    elem_relay[gy] = elem_ref[gy]
    dir_relay[gx] = dir_ref[gx]
    lax.fori_loop(FIRST, SECOND, gather, 0, unroll=2)
    settle(elem_relay, ny - 1, elem_send.at[0], elem_recv.at[0])
    settle(dir_relay, nx - 1, dir_send.at[0], dir_recv.at[0])
    for other in column_peers:
        remote(
            elem_relay.at[:, other[0]], elem_in.at[gx], elem_send.at[1], elem_recv.at[1], other
        ).start()
    for other in row_peers:
        remote(
            dir_relay.at[:, other[1]], dir_in.at[gy], dir_send.at[1], dir_recv.at[1], other
        ).start()
    elem_in[gx] = elem_relay[:, gx]
    dir_in[gy] = dir_relay[:, gy]
    pl.semaphore_wait(all_in, nx - 1)
    near = [
        remote(src, dst, near_send.at[q], near_recv.at[q], to)
        for q, (src, dst, to) in enumerate(moves)
    ]
    for copy in near:
        copy.start()
    lax.fori_loop(SECOND, blocks, gather, 0, unroll=2)

    def fill(o):
        window, valid = cut(starts_ref, o)
        return jnp.where(valid, window(val_s), 0.0)[0:4]

    value_in[me] = fill(me)

    def send_values(first, number, lot):
        others = [lax.rem(me + first + r, owners) for r in range(number)]
        for other in others:
            value_s[other] = fill(other)
        for other in others:
            remote(
                value_s.at[other], value_in.at[me], value_send, value_recv.at[lot], place(other)
            ).start()

    def send_group(g, carry):
        send_values(1 + GROUP * g, GROUP, g // (LOT // GROUP))
        return carry

    groups = (owners - 1) // GROUP
    lots = owners // LOT
    lax.fori_loop(0, groups, send_group, 0)
    send_values(1 + GROUP * groups, owners - 1 - GROUP * groups, lots - 1)

    for copy in near:
        copy.wait()

    tension(displacement_ref, rim_s, nodes_ref, grads_ref, area_ref, tension_s)
    pass_on(post_ref, solid_ref, x_up_out, x_down_out, y_up_out, y_down_out, corner_out, popul_out)
    settle(elem_in, nx - 1, elem_send.at[1], elem_recv.at[1])
    settle(dir_in, ny - 1, dir_send.at[1], dir_recv.at[1])
    acc[...] = jnp.zeros_like(acc)

    def arrived(number, lot):
        part = value_in.at[pl.ds(0, number)]
        remote(part, part, value_send, value_recv.at[lot], (right, gy)).wait_recv()

    def add_lot(lot):
        values, elems, ways = [], [], []
        for r in range(LOT):
            source = lax.rem(me + 2 * owners - (LOT * lot + r + 1), owners)
            x, y = place(source)
            values.append(value_in[source])
            elems.append(elem_in[x, y])
            ways.append(dir_in[y, x])
        v, elem, way = [
            jnp.concatenate([x[r : r + 1] for x in group for r in range(4)], axis=1)
            for group in (values, elems, ways)
        ]
        bit = jnp.left_shift(jnp.ones_like(way), way)
        parts = []
        for k in range(3):
            plus = sum(1 << i for i in range(19) if SPEEDS[i][k] == 1)
            minus = sum(1 << i for i in range(19) if SPEEDS[i][k] == -1)
            part = jnp.where((bit & plus) != 0, v, jnp.where((bit & minus) != 0, -v, 0.0))
            parts.extend(halves(part))
        left = jnp.concatenate(spread_rows(parts, elem >> 7, 32), axis=0)
        acc[...] += lax.dot_general(
            left, one_hot(elem & 127, 128), (((1,), (1,)), ((), ())), preferred_element_type=F32
        )

    def take_lot(lot, carry):
        arrived(LOT, lot)
        add_lot(lot)
        return carry

    lax.fori_loop(0, lots - 1, take_lot, 0)
    arrived(LOT - 1, lots - 1)
    add_lot(lots - 1)

    forces = [acc[64 * k : 64 * k + 32] + acc[64 * k + 32 : 64 * k + 64] for k in range(3)]
    for h in range(32):
        at = slice(128 * h, 128 * h + 128)
        lines = [f[h : h + 1] for f in forces]
        force_out[:, at] = jnp.concatenate(lines, axis=0)
        load_s[:, at] = sum(normal_ref[k : k + 1, at] * lines[k] for k in range(3)) / 3.0
    load = load_s[...]
    node = node_sums(nodes_ref, [load - tension_s[j : j + 1] for j in range(3)])
    back_s[...] = node[16:20]
    back = remote(back_s, return_s, back_send, back_recv, place(lax.rem(me + 1, owners)))
    back.start()
    sent = value_s.at[pl.ds(0, owners - 1)]
    remote(sent, sent, value_send, value_recv.at[0], (right, gy)).wait_send()
    back.wait()
    returned = jnp.concatenate([return_s[...], jnp.zeros((12, 128), F32)], axis=0)
    speed = velocity_ref[...] + time_step * (node[0:16] + returned) / mass_ref[...]
    velocity_out[...] = speed
    displacement_out[...] = displacement_ref[...] + time_step * speed


SPAN = 1024


def node_sums(nodes_ref, rows):
    total = jnp.zeros((64, 128), F32)
    for j in range(3):
        for b in range(nodes_ref.shape[1] // SPAN):
            at = slice(SPAN * b, SPAN * b + SPAN)
            n = nodes_ref[j : j + 1, at]
            left = jnp.concatenate(spread_rows(halves(rows[j][:, at]), n >> 7, 32), axis=0)
            total = total + lax.dot_general(
                left, one_hot(n & 127, 128), (((1,), (1,)), ((), ())), preferred_element_type=F32
            )
    return total[0:32] + total[32:64]


def tension(displacement_ref, rim_ref, nodes_ref, grads_ref, area_ref, tension_ref):
    field = jnp.concatenate([displacement_ref[...], rim_ref[...], jnp.zeros((12, 128), F32)], axis=0)
    table = jnp.concatenate(halves(field), axis=0)
    values = []
    for j in range(3):
        pieces = []
        for b in range(nodes_ref.shape[1] // SPAN):
            n = nodes_ref[j : j + 1, SPAN * b : SPAN * b + SPAN]
            found = jnp.dot(table, one_hot(n & 127, 128), preferred_element_type=F32)
            both = found[0:24] + found[32:56]
            rows = lax.broadcasted_iota(jnp.int32, both.shape, 0)
            pieces.append(jnp.sum(jnp.where(rows == (n >> 7), both, 0.0), axis=0, keepdims=True))
        values.append(jnp.concatenate(pieces, axis=1))
    g = [grads_ref[k : k + 1] for k in range(6)]
    area = area_ref[...]
    slope_x = area * (g[0] * values[0] + g[2] * values[1] + g[4] * values[2])
    slope_y = area * (g[1] * values[0] + g[3] * values[1] + g[5] * values[2])
    for j in range(3):
        tension_ref[j : j + 1] = g[2 * j] * slope_x + g[2 * j + 1] * slope_y


def pass_on(
    post_ref, solid_ref, x_up_ref, x_down_ref, y_up_ref, y_down_ref, corner_ref, out_ref
):
    is_solid = solid_ref[...] != 0
    rows, cols = is_solid.shape
    height = lax.broadcasted_iota(jnp.int32, (rows, cols), 1) % NZ
    lower = lax.broadcasted_iota(jnp.int32, (rows, 128), 1) < NZ

    def marked(value, solid):
        return jnp.where(solid != 0.0, BLANK, value)

    for i in range(19):
        cx, cy, cz = SPEEDS[i]
        if i == 0:
            out_ref[0] = post_ref[0]
            continue
        value = jnp.where(is_solid, BLANK, post_ref[i])

        def moved(core, first, last):
            if cx == 1:
                return jnp.concatenate([first(), core[0 : rows - 1]], axis=0)
            if cx == -1:
                return jnp.concatenate([core[1:rows], last()], axis=0)
            return core

        def x_edge(ref, names):
            q = names.index(i)
            return marked(ref[q : q + 1], ref[5:6])

        def corner():
            return marked(corner_ref[i - 7, 0:1], corner_ref[i - 7, 1:2])

        value = moved(value, lambda: x_edge(x_up_ref, X_UP), lambda: x_edge(x_down_ref, X_DOWN))
        if cy != 0:
            ref, names = (y_up_ref, Y_UP) if cy == 1 else (y_down_ref, Y_DOWN)
            edge = moved(marked(ref[names.index(i)], ref[5]), corner, corner)
            edge = pltpu.roll(edge, NZ, 1)
            value = pltpu.roll(value, NZ if cy == 1 else cols - NZ, 1)
            if cy == 1:
                value = jnp.concatenate(
                    [jnp.where(lower, edge, value[:, 0:128]), value[:, 128:]], axis=1
                )
            else:
                value = jnp.concatenate(
                    [value[:, : cols - 128], jnp.where(lower, value[:, cols - 128 :], edge)], axis=1
                )
        if cz != 0:
            value = pltpu.roll(value, 1 if cz == 1 else cols - 1, 1)
            blocked = (value == BLANK) | (height == (0 if cz == 1 else NZ - 1))
        else:
            blocked = value == BLANK
        value = jnp.where(blocked, post_ref[OPP[i]], value)
        out_ref[i] = jnp.where(is_solid, post_ref[i], value)


def store_kernel(*refs):
    count = (len(refs) - 1) // 2
    sems = refs[-1]
    copies = [
        pltpu.make_async_copy(refs[q], refs[count + q], sems.at[q]) for q in range(count)
    ]
    for copy in copies:
        copy.start()
    for copy in copies:
        copy.wait()


def call(kernel, out_shape, scratch=(), n_vmem=0, n_smem=0, smem_out=0, space_out=pltpu.VMEM, **params):
    spaces = [pltpu.SMEM] * n_smem + [pltpu.VMEM] * n_vmem
    outs = [pltpu.SMEM] * smem_out + [space_out] * (len(out_shape) - smem_out)
    return pl.pallas_call(
        kernel,
        out_shape=out_shape,
        in_specs=[pl.BlockSpec(memory_space=space) for space in spaces],
        out_specs=tuple(pl.BlockSpec(memory_space=space) for space in outs),
        scratch_shapes=list(scratch),
        compiler_params=pltpu.CompilerParams(vmem_limit_bytes=VMEM, **params),
    )


def on_device(
    populations,
    solid,
    link_cell,
    link_dir,
    link_owner,
    link_elem,
    elem_nodes,
    elem_grads,
    elem_area,
    elem_normal,
    node_mass,
    displacement,
    velocity,
):
    owners = lax.axis_size(("gx", "gy"))
    elements = elem_nodes.shape[1]
    rows, cols = solid.shape
    nodal = [x.reshape(-1, 128) for x in (displacement, velocity, node_mass)]

    def f32(*shape):
        return jax.ShapeDtypeStruct(shape, F32)

    halo_shapes = (f32(6, cols), f32(6, cols), f32(6, rows, 128), f32(6, rows, 128), f32(4, 2, 128))
    def i32(*shape):
        return jax.ShapeDtypeStruct(shape, jnp.int32)

    nx, ny = lax.axis_size("gx"), lax.axis_size("gy")
    owner = lax.optimization_barrier(link_owner.reshape(-1))
    key, code = lax.sort(
        (owner * elements + link_elem, link_dir * (rows * cols) + link_cell), num_keys=1, is_stable=False
    )
    key, code = key.reshape(-1, 128), code.reshape(-1, 128)
    count = key.shape[0]
    starts, elem, way = call(
        cut_kernel,
        (i32(8, 128), i32(ny, nx, 4, 128), i32(nx, ny, 4, 128)),
        scratch=[
            pltpu.VMEM((count + 8, 128), jnp.int32),
            pltpu.VMEM((count + 8, 128), jnp.int32),
            pltpu.VMEM((8, 128), jnp.int32),
            pltpu.SemaphoreType.DMA,
        ],
        n_vmem=2,
        smem_out=1,
    )(key, code)

    post, table, *rest = call(
        collide_kernel,
        (
            f32(*populations.shape),
            jax.ShapeDtypeStruct((576, 512), BF16),
            *halo_shapes,
            f32(16, 128),
            i32(8, 128),
        ),
        n_vmem=4,
    )(populations, solid, nodal[0], starts)
    halo, (field, starts) = rest[:5], rest[5:]

    results = call(
        exchange_kernel,
        (f32(*populations.shape), f32(3, elements), f32(16, 128), f32(16, 128)),
        scratch=[
            *[pltpu.VMEM(shape.shape, F32) for shape in halo_shapes],
            pltpu.VMEM((RIM // 128, 128), F32),
            pltpu.VMEM((136, 128), F32),
            pltpu.VMEM((owners, 4, 128), F32),
            pltpu.VMEM((owners, 4, 128), F32),
            pltpu.VMEM((ny, nx, 4, 128), jnp.int32),
            pltpu.VMEM((nx, ny, 4, 128), jnp.int32),
            pltpu.VMEM((nx, ny, 4, 128), jnp.int32),
            pltpu.VMEM((ny, nx, 4, 128), jnp.int32),
            pltpu.VMEM((3, elements), F32),
            pltpu.VMEM((1, elements), F32),
            pltpu.VMEM((192, 128), F32),
            pltpu.VMEM((RIM // 128, 128), F32),
            pltpu.VMEM((RIM // 128, 128), F32),
            pltpu.SemaphoreType.REGULAR,
            pltpu.SemaphoreType.DMA((9,)),
            pltpu.SemaphoreType.DMA((9,)),
            pltpu.SemaphoreType.DMA((2,)),
            pltpu.SemaphoreType.DMA((2,)),
            pltpu.SemaphoreType.DMA((2,)),
            pltpu.SemaphoreType.DMA((2,)),
            pltpu.SemaphoreType.DMA,
            pltpu.SemaphoreType.DMA((owners // LOT,)),
            pltpu.SemaphoreType.DMA,
            pltpu.SemaphoreType.DMA,
        ],
        n_smem=1,
        n_vmem=18,
        collective_id=0,
        has_side_effects=True,
    )(
        starts,
        code,
        table,
        elem,
        way,
        *halo,
        field,
        elem_nodes,
        elem_grads,
        elem_area.reshape(1, -1),
        elem_normal,
        *nodal[1:],
        post,
        solid,
    )

    populations_out, element_force, displacement_out, velocity_out = call(
        store_kernel,
        tuple(f32(*x.shape) for x in results),
        scratch=[pltpu.SemaphoreType.DMA((4,))],
        n_vmem=4,
        space_out=pltpu.HBM,
    )(*results)
    return (populations_out, element_force, displacement_out.reshape(-1), velocity_out.reshape(-1))


def solution(mesh):
    in_specs = (
        P(None, "gx", "gy"),
        P("gx", "gy"),
        P(("gx", "gy")),
        P(("gx", "gy")),
        P(("gx", "gy"), None),
        P(("gx", "gy")),
        P(None, ("gx", "gy")),
        P(None, ("gx", "gy")),
        P(("gx", "gy")),
        P(None, ("gx", "gy")),
        P(("gx", "gy")),
        P(("gx", "gy")),
        P(("gx", "gy")),
    )
    out_specs = (P(None, "gx", "gy"), P(None, ("gx", "gy")), P(("gx", "gy")), P(("gx", "gy")))
    return jax.shard_map(
        on_device, mesh=mesh, in_specs=in_specs, out_specs=out_specs, check_vma=False
    )
```

```python
import functools

import jax
import jax.numpy as jnp
from jax import lax
from jax.experimental import pallas as pl
from jax.experimental.pallas import tpu as pltpu
from jax.sharding import PartitionSpec as P

NZ = 64
RIM = 512
BLANK = -1e30

SPEEDS = [
    (0, 0, 0),
    (1, 0, 0),
    (-1, 0, 0),
    (0, 1, 0),
    (0, -1, 0),
    (0, 0, 1),
    (0, 0, -1),
    (1, 1, 0),
    (-1, -1, 0),
    (1, -1, 0),
    (-1, 1, 0),
    (1, 0, 1),
    (-1, 0, -1),
    (1, 0, -1),
    (-1, 0, 1),
    (0, 1, 1),
    (0, -1, -1),
    (0, 1, -1),
    (0, -1, 1),
]
WEIGHTS = [1.0 / 3.0] + [1.0 / 18.0] * 6 + [1.0 / 36.0] * 12
OPP = [0, 2, 1, 4, 3, 6, 5, 8, 7, 10, 9, 12, 11, 14, 13, 16, 15, 18, 17]
X_UP = [i for i in range(19) if SPEEDS[i][0] == 1]
X_DOWN = [i for i in range(19) if SPEEDS[i][0] == -1]
Y_UP = [i for i in range(19) if SPEEDS[i][1] == 1]
Y_DOWN = [i for i in range(19) if SPEEDS[i][1] == -1]
relax_time = 0.8
time_step = 0.5
VMEM = 48 * 1024 * 1024
F32 = jnp.float32
BF16 = jnp.bfloat16
MESH = pl.DeviceIdType.MESH
FIRST = 4
SECOND = 12
GROUP = 8
LOT = 32


def halves(x):
    high = x.astype(BF16)
    return high, (x - high.astype(F32)).astype(BF16)


def signed_sum(terms):
    plus = [v for s, v in terms if s > 0]
    minus = [v for s, v in terms if s < 0]
    return functools.reduce(jnp.add, plus) - functools.reduce(jnp.add, minus)


def signed_sum_any(terms):
    total = None
    for s, v in terms:
        if total is None:
            total = v if s > 0 else -v
        else:
            total = total + v if s > 0 else total - v
    return total


def one_hot(index, size):
    rows = lax.broadcasted_iota(jnp.int16, (size, index.shape[1]), 0)
    return jnp.where(rows == index.astype(jnp.int16), jnp.ones((), BF16), jnp.zeros((), BF16))


def spread_rows(value_rows, index, size):
    rows = lax.broadcasted_iota(jnp.int16, (size, index.shape[1]), 0)
    mine = rows == index.astype(jnp.int16)
    return [jnp.where(mine, v, jnp.zeros((), BF16)) for v in value_rows]


def cut(starts_ref, o):
    lanes = lax.broadcasted_iota(jnp.int32, (8, 128), 1)
    subs = lax.broadcasted_iota(jnp.int32, (8, 128), 0)
    base = starts_ref[0, o]
    number = starts_ref[1, o] - base
    first = base >> 7
    offset = base & 127
    near = lanes < 128 - offset

    def window(ref):
        x = pltpu.roll(ref[pl.ds(first, 8), :], (128 - offset) & 127, 1)
        return jnp.where(near, x, pltpu.roll(x, 7, 0))

    return window, subs * 128 + lanes < number


def find_starts(owner):
    last = owner.T[127:128]
    lanes = lax.broadcasted_iota(jnp.int32, (1, 128), 1)
    previous = jnp.where(lanes == 0, -1.0, pltpu.roll(last, 1, 1))
    wanted = lax.broadcasted_iota(jnp.int32, (128, 128), 0).astype(F32)
    full = last < wanted
    split = jnp.where((last >= wanted) & (previous < wanted), 1.0, 0.0).astype(BF16)
    row = jnp.dot(split, (owner - 128.0).astype(BF16), preferred_element_type=F32)
    before = jnp.where(full, 128.0, 0.0) + jnp.where(row < wanted - 128.0, 1.0, 0.0)
    starts = lax.dot_general(
        jnp.ones((8, 128), BF16),
        before.astype(BF16),
        (((1,), (1,)), ((), ())),
        preferred_element_type=F32,
    ).astype(jnp.int32)
    lanes = lax.broadcasted_iota(jnp.int32, (8, 128), 1)
    subs = lax.broadcasted_iota(jnp.int32, (8, 128), 0)
    ends = jnp.where(lanes == 127, 128 * 128, pltpu.roll(starts, 127, 1))
    return jnp.where(subs == 0, starts, ends)


def cut_kernel(key_ref, code_ref, starts_ref, elem_ref, dir_ref, elem_s, dir_s, starts_v, sem):
    starts_v[...] = find_starts((key_ref[...] >> 12).astype(F32))
    copy = pltpu.make_async_copy(starts_v, starts_ref, sem)
    copy.start()
    count = key_ref.shape[0]
    elem_s[0:count, :] = key_ref[...] & 4095
    dir_s[0:count, :] = code_ref[...] >> 13
    elem_s[count : count + 8, :] = jnp.zeros((8, 128), jnp.int32)
    dir_s[count : count + 8, :] = jnp.zeros((8, 128), jnp.int32)
    copy.wait()
    ny, nx = elem_ref.shape[:2]

    def spread(o, carry):
        window, _ = cut(starts_ref, o)
        x, y = o // ny, lax.rem(o, ny)
        elem_ref[y, x] = window(elem_s)[0:4]
        dir_ref[x, y] = window(dir_s)[0:4]
        return carry

    lax.fori_loop(0, nx * ny, spread, 0, unroll=16)


def collide_kernel(
    popul_ref,
    solid_ref,
    displacement_ref,
    starts_ref,
    post_ref,
    table_ref,
    x_up_ref,
    x_down_ref,
    y_up_ref,
    y_down_ref,
    corner_ref,
    field_out,
    starts_out,
):
    rows, cols = solid_ref.shape
    field_out[...] = displacement_ref[...]
    starts_out[...] = starts_ref[...]
    for t in range(cols // 128):
        at = pl.ds(128 * t, 128)
        f = [popul_ref[i, :, at] for i in range(19)]
        is_solid = solid_ref[:, at] != 0
        density = functools.reduce(jnp.add, f)
        inverse = 1.0 / density
        flow = [
            signed_sum([(SPEEDS[i][k], f[i]) for i in range(19) if SPEEDS[i][k] != 0]) * inverse
            for k in range(3)
        ]
        square = flow[0] * flow[0] + flow[1] * flow[1] + flow[2] * flow[2]
        rest = 1.0 - 1.5 * square
        keep = 1.0 - 1.0 / relax_time
        for i in range(19):
            if i != 0 and OPP[i] < i:
                continue
            scaled = (WEIGHTS[i] / relax_time) * density
            if i == 0:
                new = keep * f[0] + scaled * rest
                post_ref[0, :, at] = jnp.where(is_solid, f[0], new)
                continue
            along = signed_sum_any([(SPEEDS[i][k], flow[k]) for k in range(3) if SPEEDS[i][k] != 0])
            even = scaled * (rest + 4.5 * along * along)
            odd = scaled * (3.0 * along)
            j = OPP[i]
            post_ref[i, :, at] = jnp.where(is_solid, f[i], keep * f[i] + (even + odd))
            post_ref[j, :, at] = jnp.where(is_solid, f[j], keep * f[j] + (even - odd))
    for pair in range(9):
        block = jnp.concatenate(
            [
                post_ref[d, :, 128 * t : 128 * t + 128]
                for d in (1 + 2 * pair, 2 + 2 * pair)
                for t in range(cols // 128)
            ],
            axis=0,
        )
        turned = block.T
        rolled = pltpu.roll(turned, 64, 1)
        lower = lax.broadcasted_iota(jnp.int32, (16, 128), 1) < 64
        for second in range(2):
            near, far = (rolled, turned) if second else (turned, rolled)
            row = 16 * (2 * pair + second)
            for p in range(4):
                piece = jnp.where(lower, near[32 * p : 32 * p + 16], far[32 * p + 16 : 32 * p + 32])
                high, low = halves(2.0 * piece)
                table_ref[row : row + 16, 128 * p : 128 * p + 128] = high
                table_ref[288 + row : 304 + row, 128 * p : 128 * p + 128] = low

    flag = solid_ref[...].astype(F32)
    for q in range(5):
        x_up_ref[q : q + 1] = post_ref[X_UP[q], rows - 1 : rows]
        x_down_ref[q : q + 1] = post_ref[X_DOWN[q], 0:1]
        y_up_ref[q] = post_ref[Y_UP[q], :, cols - 128 : cols]
        y_down_ref[q] = post_ref[Y_DOWN[q], :, 0:128]
    x_up_ref[5:6] = flag[rows - 1 : rows]
    x_down_ref[5:6] = flag[0:1]
    y_up_ref[5] = flag[:, cols - 128 : cols]
    y_down_ref[5] = flag[:, 0:128]
    for q in range(4):
        cx, cy, _ = SPEEDS[7 + q]
        row = slice(rows - 1, rows) if cx == 1 else slice(0, 1)
        lane = slice(cols - 128, cols) if cy == 1 else slice(0, 128)
        corner_ref[q, 0:1] = post_ref[7 + q, row, lane]
        corner_ref[q, 1:2] = flag[row, lane]


def exchange_kernel(
    starts_ref,
    code_ref,
    table_ref,
    elem_ref,
    dir_ref,
    x_up_ref,
    x_down_ref,
    y_up_ref,
    y_down_ref,
    corner_ref,
    displacement_ref,
    nodes_ref,
    grads_ref,
    area_ref,
    normal_ref,
    velocity_ref,
    mass_ref,
    post_ref,
    solid_ref,
    popul_out,
    force_out,
    displacement_out,
    velocity_out,
    x_up_out,
    x_down_out,
    y_up_out,
    y_down_out,
    corner_out,
    rim_s,
    val_s,
    value_s,
    value_in,
    elem_relay,
    dir_relay,
    elem_in,
    dir_in,
    tension_s,
    load_s,
    acc,
    back_s,
    return_s,
    all_in,
    near_send,
    near_recv,
    elem_send,
    elem_recv,
    dir_send,
    dir_recv,
    value_send,
    value_recv,
    back_send,
    back_recv,
):
    count = code_ref.shape[0]
    gx, gy = lax.axis_index("gx"), lax.axis_index("gy")
    nx, ny = lax.axis_size("gx"), lax.axis_size("gy")
    owners = nx * ny
    me = gx * ny + gy

    def place(other):
        return (other // ny, lax.rem(other, ny))

    barrier = pltpu.get_barrier_semaphore()

    row_peers = [(gx, lax.rem(gy + d, ny)) for d in range(1, ny)]
    column_peers = [(lax.rem(gx + d, nx), gy) for d in range(1, nx)]
    for other in row_peers + column_peers:
        pl.semaphore_signal(barrier, inc=1, device_id=other, device_id_type=MESH)

    span = 8

    def gather(b, carry):
        code = code_ref[pl.ds(pl.multiple_of(span * b, span), span), :]
        code = jnp.concatenate([code[r : r + 1] for r in range(span)], axis=1)
        cell = code & 8191
        column = ((cell >> 4) & 7) * 64 + ((cell >> 7) & 7) * 8 + (cell >> 10)
        row = ((code >> 13) - 1) * 16 + (cell & 15)
        hot = one_hot(column, table_ref.shape[1])
        found = jnp.dot(table_ref[...], hot, preferred_element_type=F32)
        both = found[0:288] + found[288:576]
        rows = lax.broadcasted_iota(jnp.int32, both.shape, 0)
        got = jnp.sum(jnp.where(rows == row, both, 0.0), axis=0, keepdims=True)
        for r in range(span):
            val_s[pl.ds(span * b + r, 1), :] = got[:, 128 * r : 128 * r + 128]
        return carry

    blocks = count // span
    val_s[count : count + 8, :] = jnp.zeros((8, 128), F32)

    lax.fori_loop(0, FIRST, gather, 0, unroll=2)
    pl.semaphore_wait(barrier, nx + ny - 2)
    for other in column_peers:
        pl.semaphore_signal(all_in, inc=1, device_id=other, device_id_type=MESH)

    right, left = lax.rem(gx + 1, nx), lax.rem(gx + nx - 1, nx)
    above, below = lax.rem(gy + 1, ny), lax.rem(gy + ny - 1, ny)
    moves = [
        (x_up_ref, x_up_out, (right, gy)),
        (x_down_ref, x_down_out, (left, gy)),
        (y_up_ref, y_up_out, (gx, above)),
        (y_down_ref, y_down_out, (gx, below)),
        (corner_ref.at[0], corner_out.at[0], (right, above)),
        (corner_ref.at[1], corner_out.at[1], (left, below)),
        (corner_ref.at[2], corner_out.at[2], (right, below)),
        (corner_ref.at[3], corner_out.at[3], (left, above)),
        (displacement_ref.at[0 : RIM // 128], rim_s, place(lax.rem(me + owners - 1, owners))),
    ]
    def remote(src, dst, send_sem, recv_sem, other):
        return pltpu.make_async_remote_copy(
            src_ref=src,
            dst_ref=dst,
            send_sem=send_sem,
            recv_sem=recv_sem,
            device_id=other,
            device_id_type=MESH,
        )

    def settle(buffer, number, send_sem, recv_sem):
        part = buffer.at[pl.ds(0, number)]
        remote(part, part, send_sem, recv_sem, (right, gy)).wait()

    for other in row_peers:
        remote(elem_ref.at[other[1]], elem_relay.at[gy], elem_send.at[0], elem_recv.at[0], other).start()
    for other in column_peers:
        remote(dir_ref.at[other[0]], dir_relay.at[gx], dir_send.at[0], dir_recv.at[0], other).start()
    elem_relay[gy] = elem_ref[gy]
    dir_relay[gx] = dir_ref[gx]
    lax.fori_loop(FIRST, SECOND, gather, 0, unroll=2)
    settle(elem_relay, ny - 1, elem_send.at[0], elem_recv.at[0])
    settle(dir_relay, nx - 1, dir_send.at[0], dir_recv.at[0])
    for other in column_peers:
        remote(
            elem_relay.at[:, other[0]], elem_in.at[gx], elem_send.at[1], elem_recv.at[1], other
        ).start()
    for other in row_peers:
        remote(
            dir_relay.at[:, other[1]], dir_in.at[gy], dir_send.at[1], dir_recv.at[1], other
        ).start()
    elem_in[gx] = elem_relay[:, gx]
    dir_in[gy] = dir_relay[:, gy]
    pl.semaphore_wait(all_in, nx - 1)
    near = [
        remote(src, dst, near_send.at[q], near_recv.at[q], to)
        for q, (src, dst, to) in enumerate(moves)
    ]
    for copy in near:
        copy.start()
    lax.fori_loop(SECOND, blocks, gather, 0, unroll=2)

    def fill(o):
        window, valid = cut(starts_ref, o)
        return jnp.where(valid, window(val_s), 0.0)[0:4]

    value_in[me] = fill(me)

    def send_values(first, number, lot):
        others = [lax.rem(me + first + r, owners) for r in range(number)]
        for other in others:
            value_s[other] = fill(other)
        for other in others:
            remote(
                value_s.at[other], value_in.at[me], value_send, value_recv.at[lot], place(other)
            ).start()

    def send_group(g, carry):
        send_values(1 + GROUP * g, GROUP, g // (LOT // GROUP))
        return carry

    groups = (owners - 1) // GROUP
    lots = owners // LOT
    lax.fori_loop(0, groups, send_group, 0)
    send_values(1 + GROUP * groups, owners - 1 - GROUP * groups, lots - 1)

    for copy in near:
        copy.wait()

    tension(displacement_ref, rim_s, nodes_ref, grads_ref, area_ref, tension_s)
    pass_on(post_ref, solid_ref, x_up_out, x_down_out, y_up_out, y_down_out, corner_out, popul_out)
    settle(elem_in, nx - 1, elem_send.at[1], elem_recv.at[1])
    settle(dir_in, ny - 1, dir_send.at[1], dir_recv.at[1])
    acc[...] = jnp.zeros_like(acc)

    def arrived(number, lot):
        part = value_in.at[pl.ds(0, number)]
        remote(part, part, value_send, value_recv.at[lot], (right, gy)).wait_recv()

    def add_lot(lot):
        values, elems, ways = [], [], []
        for r in range(LOT):
            source = lax.rem(me + 2 * owners - (LOT * lot + r + 1), owners)
            x, y = place(source)
            values.append(value_in[source])
            elems.append(elem_in[x, y])
            ways.append(dir_in[y, x])
        v, elem, way = [
            jnp.concatenate([x[r : r + 1] for x in group for r in range(4)], axis=1)
            for group in (values, elems, ways)
        ]
        bit = jnp.left_shift(jnp.ones_like(way), way)
        parts = []
        for k in range(3):
            plus = sum(1 << i for i in range(19) if SPEEDS[i][k] == 1)
            minus = sum(1 << i for i in range(19) if SPEEDS[i][k] == -1)
            part = jnp.where((bit & plus) != 0, v, jnp.where((bit & minus) != 0, -v, 0.0))
            parts.extend(halves(part))
        left = jnp.concatenate(spread_rows(parts, elem >> 7, 32), axis=0)
        acc[...] += lax.dot_general(
            left, one_hot(elem & 127, 128), (((1,), (1,)), ((), ())), preferred_element_type=F32
        )

    def take_lot(lot, carry):
        arrived(LOT, lot)
        add_lot(lot)
        return carry

    lax.fori_loop(0, lots - 1, take_lot, 0)
    arrived(LOT - 1, lots - 1)
    add_lot(lots - 1)

    forces = [acc[64 * k : 64 * k + 32] + acc[64 * k + 32 : 64 * k + 64] for k in range(3)]
    for h in range(32):
        at = slice(128 * h, 128 * h + 128)
        lines = [f[h : h + 1] for f in forces]
        force_out[:, at] = jnp.concatenate(lines, axis=0)
        load_s[:, at] = sum(normal_ref[k : k + 1, at] * lines[k] for k in range(3)) / 3.0
    load = load_s[...]
    node = node_sums(nodes_ref, [load - tension_s[j : j + 1] for j in range(3)])
    back_s[...] = node[16:20]
    back = remote(back_s, return_s, back_send, back_recv, place(lax.rem(me + 1, owners)))
    back.start()
    sent = value_s.at[pl.ds(0, owners - 1)]
    remote(sent, sent, value_send, value_recv.at[0], (right, gy)).wait_send()
    back.wait()
    returned = jnp.concatenate([return_s[...], jnp.zeros((12, 128), F32)], axis=0)
    speed = velocity_ref[...] + time_step * (node[0:16] + returned) / mass_ref[...]
    velocity_out[...] = speed
    displacement_out[...] = displacement_ref[...] + time_step * speed


SPAN = 1024


def node_sums(nodes_ref, rows):
    total = jnp.zeros((64, 128), F32)
    for j in range(3):
        for b in range(nodes_ref.shape[1] // SPAN):
            at = slice(SPAN * b, SPAN * b + SPAN)
            n = nodes_ref[j : j + 1, at]
            left = jnp.concatenate(spread_rows(halves(rows[j][:, at]), n >> 7, 32), axis=0)
            total = total + lax.dot_general(
                left, one_hot(n & 127, 128), (((1,), (1,)), ((), ())), preferred_element_type=F32
            )
    return total[0:32] + total[32:64]


def tension(displacement_ref, rim_ref, nodes_ref, grads_ref, area_ref, tension_ref):
    field = jnp.concatenate([displacement_ref[...], rim_ref[...], jnp.zeros((12, 128), F32)], axis=0)
    table = jnp.concatenate(halves(field), axis=0)
    values = []
    for j in range(3):
        pieces = []
        for b in range(nodes_ref.shape[1] // SPAN):
            n = nodes_ref[j : j + 1, SPAN * b : SPAN * b + SPAN]
            found = jnp.dot(table, one_hot(n & 127, 128), preferred_element_type=F32)
            both = found[0:24] + found[32:56]
            rows = lax.broadcasted_iota(jnp.int32, both.shape, 0)
            pieces.append(jnp.sum(jnp.where(rows == (n >> 7), both, 0.0), axis=0, keepdims=True))
        values.append(jnp.concatenate(pieces, axis=1))
    g = [grads_ref[k : k + 1] for k in range(6)]
    area = area_ref[...]
    slope_x = area * (g[0] * values[0] + g[2] * values[1] + g[4] * values[2])
    slope_y = area * (g[1] * values[0] + g[3] * values[1] + g[5] * values[2])
    for j in range(3):
        tension_ref[j : j + 1] = g[2 * j] * slope_x + g[2 * j + 1] * slope_y


def pass_on(
    post_ref, solid_ref, x_up_ref, x_down_ref, y_up_ref, y_down_ref, corner_ref, out_ref
):
    is_solid = solid_ref[...] != 0
    rows, cols = is_solid.shape
    height = lax.broadcasted_iota(jnp.int32, (rows, cols), 1) % NZ
    lower = lax.broadcasted_iota(jnp.int32, (rows, 128), 1) < NZ

    def marked(value, solid):
        return jnp.where(solid != 0.0, BLANK, value)

    for i in range(19):
        cx, cy, cz = SPEEDS[i]
        if i == 0:
            out_ref[0] = post_ref[0]
            continue
        value = jnp.where(is_solid, BLANK, post_ref[i])

        def moved(core, first, last):
            if cx == 1:
                return jnp.concatenate([first(), core[0 : rows - 1]], axis=0)
            if cx == -1:
                return jnp.concatenate([core[1:rows], last()], axis=0)
            return core

        def x_edge(ref, names):
            q = names.index(i)
            return marked(ref[q : q + 1], ref[5:6])

        def corner():
            return marked(corner_ref[i - 7, 0:1], corner_ref[i - 7, 1:2])

        value = moved(value, lambda: x_edge(x_up_ref, X_UP), lambda: x_edge(x_down_ref, X_DOWN))
        if cy != 0:
            ref, names = (y_up_ref, Y_UP) if cy == 1 else (y_down_ref, Y_DOWN)
            edge = moved(marked(ref[names.index(i)], ref[5]), corner, corner)
            edge = pltpu.roll(edge, NZ, 1)
            value = pltpu.roll(value, NZ if cy == 1 else cols - NZ, 1)
            if cy == 1:
                value = jnp.concatenate(
                    [jnp.where(lower, edge, value[:, 0:128]), value[:, 128:]], axis=1
                )
            else:
                value = jnp.concatenate(
                    [value[:, : cols - 128], jnp.where(lower, value[:, cols - 128 :], edge)], axis=1
                )
        if cz != 0:
            value = pltpu.roll(value, 1 if cz == 1 else cols - 1, 1)
            blocked = (value == BLANK) | (height == (0 if cz == 1 else NZ - 1))
        else:
            blocked = value == BLANK
        value = jnp.where(blocked, post_ref[OPP[i]], value)
        out_ref[i] = jnp.where(is_solid, post_ref[i], value)


def store_kernel(*refs):
    count = (len(refs) - 1) // 2
    sems = refs[-1]
    copies = [
        pltpu.make_async_copy(refs[q], refs[count + q], sems.at[q]) for q in range(count)
    ]
    for copy in copies:
        copy.start()
    for copy in copies:
        copy.wait()


def call(kernel, out_shape, scratch=(), n_vmem=0, n_smem=0, smem_out=0, space_out=pltpu.VMEM, **params):
    spaces = [pltpu.SMEM] * n_smem + [pltpu.VMEM] * n_vmem
    outs = [pltpu.SMEM] * smem_out + [space_out] * (len(out_shape) - smem_out)
    return pl.pallas_call(
        kernel,
        out_shape=out_shape,
        in_specs=[pl.BlockSpec(memory_space=space) for space in spaces],
        out_specs=tuple(pl.BlockSpec(memory_space=space) for space in outs),
        scratch_shapes=list(scratch),
        compiler_params=pltpu.CompilerParams(vmem_limit_bytes=VMEM, **params),
    )


def on_device(
    populations,
    solid,
    link_cell,
    link_dir,
    link_owner,
    link_elem,
    elem_nodes,
    elem_grads,
    elem_area,
    elem_normal,
    node_mass,
    displacement,
    velocity,
):
    owners = lax.axis_size(("gx", "gy"))
    elements = elem_nodes.shape[1]
    rows, cols = solid.shape
    nodal = [x.reshape(-1, 128) for x in (displacement, velocity, node_mass)]

    def f32(*shape):
        return jax.ShapeDtypeStruct(shape, F32)

    halo_shapes = (f32(6, cols), f32(6, cols), f32(6, rows, 128), f32(6, rows, 128), f32(4, 2, 128))
    def i32(*shape):
        return jax.ShapeDtypeStruct(shape, jnp.int32)

    nx, ny = lax.axis_size("gx"), lax.axis_size("gy")
    owner = lax.optimization_barrier(link_owner.reshape(-1))
    key, code = lax.sort(
        (owner * elements + link_elem, link_dir * (rows * cols) + link_cell), num_keys=1, is_stable=False
    )
    key, code = key.reshape(-1, 128), code.reshape(-1, 128)
    count = key.shape[0]
    starts, elem, way = call(
        cut_kernel,
        (i32(8, 128), i32(ny, nx, 4, 128), i32(nx, ny, 4, 128)),
        scratch=[
            pltpu.VMEM((count + 8, 128), jnp.int32),
            pltpu.VMEM((count + 8, 128), jnp.int32),
            pltpu.VMEM((8, 128), jnp.int32),
            pltpu.SemaphoreType.DMA,
        ],
        n_vmem=2,
        smem_out=1,
    )(key, code)

    post, table, *rest = call(
        collide_kernel,
        (
            f32(*populations.shape),
            jax.ShapeDtypeStruct((576, 512), BF16),
            *halo_shapes,
            f32(16, 128),
            i32(8, 128),
        ),
        n_vmem=4,
    )(populations, solid, nodal[0], starts)
    halo, (field, starts) = rest[:5], rest[5:]

    results = call(
        exchange_kernel,
        (f32(*populations.shape), f32(3, elements), f32(16, 128), f32(16, 128)),
        scratch=[
            *[pltpu.VMEM(shape.shape, F32) for shape in halo_shapes],
            pltpu.VMEM((RIM // 128, 128), F32),
            pltpu.VMEM((136, 128), F32),
            pltpu.VMEM((owners, 4, 128), F32),
            pltpu.VMEM((owners, 4, 128), F32),
            pltpu.VMEM((ny, nx, 4, 128), jnp.int32),
            pltpu.VMEM((nx, ny, 4, 128), jnp.int32),
            pltpu.VMEM((nx, ny, 4, 128), jnp.int32),
            pltpu.VMEM((ny, nx, 4, 128), jnp.int32),
            pltpu.VMEM((3, elements), F32),
            pltpu.VMEM((1, elements), F32),
            pltpu.VMEM((192, 128), F32),
            pltpu.VMEM((RIM // 128, 128), F32),
            pltpu.VMEM((RIM // 128, 128), F32),
            pltpu.SemaphoreType.REGULAR,
            pltpu.SemaphoreType.DMA((9,)),
            pltpu.SemaphoreType.DMA((9,)),
            pltpu.SemaphoreType.DMA((2,)),
            pltpu.SemaphoreType.DMA((2,)),
            pltpu.SemaphoreType.DMA((2,)),
            pltpu.SemaphoreType.DMA((2,)),
            pltpu.SemaphoreType.DMA,
            pltpu.SemaphoreType.DMA((owners // LOT,)),
            pltpu.SemaphoreType.DMA,
            pltpu.SemaphoreType.DMA,
        ],
        n_smem=1,
        n_vmem=18,
        collective_id=0,
        has_side_effects=True,
    )(
        starts,
        code,
        table,
        elem,
        way,
        *halo,
        field,
        elem_nodes,
        elem_grads,
        elem_area.reshape(1, -1),
        elem_normal,
        *nodal[1:],
        post,
        solid,
    )

    populations_out, element_force, displacement_out, velocity_out = call(
        store_kernel,
        tuple(f32(*x.shape) for x in results),
        scratch=[pltpu.SemaphoreType.DMA((4,))],
        n_vmem=4,
        space_out=pltpu.HBM,
    )(*results)
    return (populations_out, element_force, displacement_out.reshape(-1), velocity_out.reshape(-1))


def solution(mesh):
    in_specs = (
        P(None, "gx", "gy"),
        P("gx", "gy"),
        P(("gx", "gy")),
        P(("gx", "gy")),
        P(("gx", "gy"), None),
        P(("gx", "gy")),
        P(None, ("gx", "gy")),
        P(None, ("gx", "gy")),
        P(("gx", "gy")),
        P(None, ("gx", "gy")),
        P(("gx", "gy")),
        P(("gx", "gy")),
        P(("gx", "gy")),
    )
    out_specs = (P(None, "gx", "gy"), P(None, ("gx", "gy")), P(("gx", "gy")), P(("gx", "gy")))
    return jax.shard_map(
        on_device, mesh=mesh, in_specs=in_specs, out_specs=out_specs, check_vma=False
    )
```
